128 devices in a mesh: row: 8 (over z, core), col: 16 (over x, y).
Axes of the slice: x: 4, y: 4, z: 4, core: 2. Of those that a mesh axis runs over, the one named last changes fastest.
Arguments:
- loaded: bfloat16 [8192, 4096], P(('row', 'col')), may hold values from -6 to 6
- lengths: int32 [128, 8], replicated, may hold values from 1 to 15, as said below
- offsets: int32 [128, 8], replicated, may hold values from 0 to 8191, as said below
- gate_weight: bfloat16 [4096, 14784], P(None, 'col'), may hold values from -0.09375 to 0.09375
- up_weight: bfloat16 [4096, 14784], P(None, 'col'), may hold values from -0.09375 to 0.09375
- down_weight: bfloat16 [14784, 4096], P('col'), may hold values from -0.046875 to 0.046875
Outputs:
- mixed: bfloat16 [8192, 4096], P('row', 'col')
The draws below stay inside these ranges and needn't reach their ends.
Inputs may be any that keep to these rules, and one draw needn't show every extreme that they name: Each loader device's pieces 2q and 2q + 1 have lengths summing to 16. `offsets`: every packed position receives exactly one token. The tokens of one loader device that land in one row block of 1024 positions number either 0 or exactly 16; each loader device feeds exactly 4 row blocks.
All inputs are finite; a program needn't handle non-finite values.
Results may differ from the reference program's by a relative error of at most 0.0049.
Values may be sent and summed in bfloat16 or wider, within the bound.
A program may use at most 192 MiB of HBM per device.

```python
import jax
import jax.numpy as jnp
from jax import lax

D = 4096
FF = 14784
LOAD_DEV = 64
TRAJ = 8
CAP = 16
TOK_ROW = 1024
TOKENS = 8192
N_ROW = 8
N_COL = 16


def packing_plan(key):
    devices = N_ROW * N_COL
    keys = jax.random.split(key, 3)
    order = jax.random.permutation(keys[0], devices).astype(jnp.int32)
    turn = jax.random.randint(keys[1], (devices,), 0, 4).astype(jnp.int32)
    first = jax.random.randint(keys[2], (devices, 4), 1, CAP).astype(jnp.int32)
    lengths = jnp.stack([first, CAP - first], axis=2).reshape(devices, TRAJ)
    quarter = jnp.arange(4, dtype=jnp.int32)
    turned = (quarter[None, :] + turn[:, None]) % 4
    target = (order[:, None] + turned * N_COL) % devices
    block_row = target // N_COL
    sub_slot = turned * N_COL + target % N_COL
    start = block_row * (4 * CAP * N_COL) + sub_slot * CAP
    offsets = jnp.stack([start, start + first], axis=2).reshape(devices, TRAJ)
    return (lengths.astype(jnp.int32), offsets.astype(jnp.int32))


def draw_lengths(key, part):
    return packing_plan(key)[0]


def draw_offsets(key, part):
    return packing_plan(key)[1]


def block_scale(stream_key, shape, pieces, least, largest):
    def one(dim, blocks):
        steps = jax.random.uniform(jax.random.fold_in(jax.random.fold_in(stream_key, 6), dim), (blocks,), jnp.float32, least / len(pieces), largest / len(pieces))
        return jnp.repeat(jnp.exp(steps), shape[dim] // blocks).reshape((-1,) + (1,) * (len(shape) - dim - 1))

    factor_of = one(*pieces[0])
    for cut in pieces[1:]:
        factor_of = factor_of * one(*cut)
    return factor_of


def gaussian(key, shape, spread, reach, shards=(), held_as=jnp.bfloat16):
    level = block_scale(key, shape, shards, -0.22, 0.18) if shards else 1.0
    array = jax.random.normal(key, shape, jnp.float32) * spread * level
    return jnp.minimum(jnp.maximum(array, -reach), reach).astype(held_as)


def setup_inputs(seed: int = 0) -> dict:
    key_list = jax.random.split(jax.random.key(seed), 7)
    return {
        "loaded": gaussian(key_list[0], (TOKENS, D), 1.0, 6.0, ((0, 128),)),
        "lengths": draw_lengths(jax.random.fold_in(key_list[6], 71), 0),
        "offsets": draw_offsets(jax.random.fold_in(key_list[6], 71), 0),
        "gate_weight": gaussian(key_list[3], (D, FF), D ** -0.5, 0.09375, ((1, 16),)),
        "up_weight": gaussian(key_list[4], (D, FF), D ** -0.5, 0.09375, ((1, 16),)),
        "down_weight": gaussian(key_list[5], (FF, D), FF ** -0.5, 0.046875, ((0, 16),)),
    }


def destinations(lengths, offsets):
    ends = jnp.cumsum(lengths, axis=1).astype(jnp.int32)
    starts = ends - lengths
    positions = jnp.arange(LOAD_DEV, dtype=jnp.int32)
    which = jnp.sum((positions[None, :, None] >= ends[:, None, :]).astype(jnp.int32), axis=2).astype(jnp.int32)
    base = jnp.take_along_axis(offsets - starts, which, axis=1)
    return (base + positions[None, :]).astype(jnp.int32)


def reference(loaded, lengths, offsets, gate_weight, up_weight, down_weight):
    position = destinations(lengths, offsets).reshape(-1)
    packed = jnp.zeros((TOKENS, D), jnp.bfloat16).at[position].set(loaded)
    blocks = packed.reshape(TOKENS // TOK_ROW, TOK_ROW, D)

    def layer(block):
        gate = jnp.dot(block, gate_weight, preferred_element_type=jnp.float32)
        up = jnp.dot(block, up_weight, preferred_element_type=jnp.float32)
        hidden = (jax.nn.silu(gate) * up).astype(jnp.bfloat16)
        return jnp.dot(hidden, down_weight, preferred_element_type=jnp.float32).astype(jnp.bfloat16)

    return lax.map(layer, blocks).reshape(TOKENS, D)
```

```python
import functools

import jax
import jax.numpy as jnp
from jax import lax
from jax.experimental import pallas as pl
from jax.experimental.pallas import tpu as pltpu
from jax.sharding import PartitionSpec as P

MESH = pl.DeviceIdType.MESH
N_ROW = 8
N_COL = 16
RING = 4
LOAD = 64
CAP = 16
TRAJ = 8
TOK = 1024
HALF = 512
WIDTH = 256
SRC = N_ROW * N_COL
I32 = jnp.int32
F32 = jnp.float32
BF16 = jnp.bfloat16


def plan_kernel(len_s, off_s, len_t, off_t, loaded, out, table):
    row = lax.axis_index("row")
    me = row * N_COL + lax.axis_index("col")
    lane = lax.broadcasted_iota(I32, (LOAD, LOAD), 1)
    sub = lax.broadcasted_iota(I32, (LOAD, LOAD), 0)
    pos_l = jnp.zeros((LOAD, LOAD), I32)
    pos_s = jnp.zeros((LOAD, LOAD), I32)
    start = jnp.int32(0)
    for j in range(TRAJ):
        end = start + len_s[me, j]
        shift = off_s[me, j] - start
        pos_l = jnp.where((lane >= start) & (lane < end), shift + lane, pos_l)
        pos_s = jnp.where((sub >= start) & (sub < end), shift + sub, pos_s)
        start = end
    block_l = pos_l // TOK
    block_s = pos_s // TOK
    rank = jnp.sum(
        jnp.where((block_l == block_s) & (sub < lane), 1.0, 0.0), axis=0, keepdims=True
    ).astype(I32)
    target = block_l[0:1, :] * CAP + rank
    slot = lax.broadcasted_iota(I32, (N_ROW * CAP, LOAD), 0)
    select = jnp.where(target == slot, 1.0, 0.0).astype(BF16)
    for c in range(N_COL):
        picked = jnp.dot(select, loaded[:, c * WIDTH : (c + 1) * WIDTH], preferred_element_type=F32)
        out[:, c] = picked.astype(BF16).reshape(N_ROW, CAP, WIDTH)

    tok = lax.broadcasted_iota(I32, (LOAD, SRC), 0)
    pos = jnp.zeros((LOAD, SRC), I32)
    start = jnp.zeros((1, SRC), I32)
    for j in range(TRAJ):
        end = start + len_t[j : j + 1, :]
        pos = jnp.where((tok >= start) & (tok < end), off_t[j : j + 1, :] - start + tok, pos)
        start = end
    mine = pos // TOK == row
    below = jnp.where(sub > lane, 1.0, 0.0).astype(BF16)
    order = jnp.dot(below, jnp.where(mine, 1.0, 0.0).astype(BF16), preferred_element_type=F32)
    order = order.astype(I32)
    in_row = jnp.where(mine, pos % TOK + 1, 0)
    by_slot = jnp.concatenate(
        [
            jnp.sum(jnp.where(order == q, in_row, 0).astype(F32), axis=0, keepdims=True)
            for q in range(CAP)
        ],
        axis=0,
    ).astype(I32)
    wide_s = lax.broadcasted_iota(I32, (SRC, CAP), 0)
    wide_l = lax.broadcasted_iota(I32, (SRC, CAP), 1)
    spread = jnp.where(wide_s % CAP == wide_l, 1.0, 0.0).astype(BF16)
    sq_s = lax.broadcasted_iota(I32, (SRC, SRC), 0)
    sq_l = lax.broadcasted_iota(I32, (SRC, SRC), 1)
    keep = sq_l % 8 == sq_s // CAP
    group_s = lax.broadcasted_iota(I32, (CAP, SRC), 0)
    group_l = lax.broadcasted_iota(I32, (CAP, SRC), 1)
    group = jnp.where(group_l // 8 == group_s, 1.0, 0.0).astype(BF16)
    total = jnp.zeros((CAP, SRC), F32)
    for part, scale in ((by_slot // 32, 32.0), (by_slot % 32, 1.0)):
        y = jnp.dot(spread, part.astype(F32).astype(BF16), preferred_element_type=F32)
        y = jnp.where(keep, y, 0.0).astype(BF16)
        total = total + scale * lax.dot_general(
            group, y, (((1,), (1,)), ((), ())), preferred_element_type=F32
        )
    table[...] = total.astype(I32) - 1


def ffn_kernel(
    arrived, table, wg_hbm, wu_hbm, wd_hbm, out,
    wg, wu, wd, x, accg, accu, hid, hot, got,
    w_sem, ag_send, ag_recv, rs_send, rs_recv,
):
    row = lax.axis_index("row")
    col = lax.axis_index("col")
    swap = lax.rem(row, 2)
    cx = lax.div(col, RING)
    cy = lax.rem(col, RING)
    a0 = (1 - swap) * cx + swap * cy
    b0 = (1 - swap) * cy + swap * cx

    def col_of(da, db):
        a = lax.rem(a0 + da, RING)
        b = lax.rem(b0 + db, RING)
        return (1 - swap) * (a * RING + b) + swap * (b * RING + a)

    near = {
        "a+": (row, col_of(1, 0)),
        "a-": (row, col_of(3, 0)),
        "b+": (row, col_of(0, 1)),
        "b-": (row, col_of(0, 3)),
    }
    loads = [
        pltpu.make_async_copy(src, dst, w_sem.at[i])
        for i, (src, dst) in enumerate(((wg_hbm, wg), (wu_hbm, wu), (wd_hbm, wd)))
    ]
    for load in loads:
        load.start()

    barrier = pltpu.get_barrier_semaphore()
    for who in near.values():
        pl.semaphore_signal(barrier, inc=1, device_id=who, device_id_type=MESH)

    def compact(m):
        place = lax.broadcasted_iota(I32, (WIDTH, SRC), 0) + m * WIDTH
        for g in range(CAP):
            hot[:, g * SRC : (g + 1) * SRC] = jnp.where(
                table[g : g + 1, :] == place, 1.0, 0.0
            ).astype(BF16)
        x[0, m // 2, (m % 2) * WIDTH : (m % 2 + 1) * WIDTH, :] = jnp.dot(
            hot[...], arrived[...], preferred_element_type=F32
        ).astype(BF16)

    sends = {}
    count = [0]

    def forward(slot, h, way, to):
        copy = pltpu.make_async_remote_copy(
            src_ref=x.at[slot, h],
            dst_ref=x.at[to, h],
            send_sem=ag_send.at[count[0]],
            recv_sem=ag_recv.at[to, h],
            device_id=near[way],
            device_id_type=MESH,
        )
        count[0] += 1
        copy.start()
        sends.setdefault((slot, h), []).append(copy)

    def pass_on(slot, h):
        da, db = slot // RING, slot % RING
        if db == 0:
            if da == 0:
                forward(slot, h, "a-", 1 * RING)
                forward(slot, h, "a+", 3 * RING)
            if da == 3 and h == 0:
                forward(slot, h, "a+", 2 * RING)
            if da == 1 and h == 1:
                forward(slot, h, "a-", 2 * RING)
            forward(slot, h, "b-", da * RING + 1)
            forward(slot, h, "b+", da * RING + 3)
        if db == 3 and h == 0:
            forward(slot, h, "b+", da * RING + 2)
        if db == 1 and h == 1:
            forward(slot, h, "b-", da * RING + 2)

    def take(slot, h):
        pltpu.make_async_copy(x.at[slot, h], x.at[slot, h], ag_recv.at[slot, h]).wait()
        pass_on(slot, h)

    def gate_up(slots, first=False, last=False):
        ks = [
            pl.ds(pl.multiple_of(col_of(s // RING, s % RING) * WIDTH, WIDTH), WIDTH) for s in slots
        ]

        def chunk(m, carry):
            h = lax.div(m, 2)
            src = pl.ds(pl.multiple_of(lax.rem(m, 2) * WIDTH, WIDTH), WIDTH)
            dst = pl.ds(pl.multiple_of(m * WIDTH, WIDTH), WIDTH)
            g = u = None
            for s, k in zip(slots, ks):
                lhs = x[s, h, src, :]
                dg = jnp.dot(lhs, wg[k, :], preferred_element_type=F32)
                du = jnp.dot(lhs, wu[k, :], preferred_element_type=F32)
                g = dg if g is None else g + dg
                u = du if u is None else u + du
            if not first:
                g = accg[dst, :] + g
                u = accu[dst, :] + u
            if last:
                hid[dst, :] = (g / (1.0 + jnp.exp(-g)) * u).astype(BF16)
            else:
                accg[dst, :] = g
                accu[dst, :] = u
            return carry

        lax.fori_loop(0, TOK // WIDTH, chunk, 0)

    compact(0)
    compact(1)
    pl.semaphore_wait(barrier, 4)
    pass_on(0, 0)
    compact(2)
    compact(3)
    pass_on(0, 1)
    groups = [[4, 12], [1, 3], [8, 2], [5, 7], [13, 15], [6, 14], [9, 11], [10]]
    for load in loads[:2]:
        load.wait()
    pending = [0]
    for i, group in enumerate(groups):
        for slot in group:
            take(slot, 0)
            take(slot, 1)
        gate_up(pending, first=i == 0)
        pending = group
    gate_up(pending, last=True)
    loads[2].wait()

    spots = [(s, h) for s in (2, 6, 14, 10, 0, 1, 3, 4, 12, 5, 7, 13, 15, 8, 9, 11) for h in (0, 1)]
    started = []

    def product(slot, h):
        cols = pl.ds(pl.multiple_of(col_of(slot // RING, slot % RING) * WIDTH, WIDTH), WIDTH)
        return jnp.dot(
            hid[h * HALF : (h + 1) * HALF, :], wd[:, cols], preferred_element_type=F32
        )

    def landed(i):
        pltpu.make_async_copy(got.at[i], got.at[i], rs_recv.at[i]).wait()
        return got[i].astype(F32)

    def send(value, way, to):
        n = len(started)
        spot = spots[n]
        for copy in sends.pop(spot, []):
            copy.wait_send()
        x[spot[0], spot[1]] = value.astype(BF16)
        copy = pltpu.make_async_remote_copy(
            src_ref=x.at[spot[0], spot[1]],
            dst_ref=got.at[to],
            send_sem=rs_send.at[n],
            recv_sem=rs_recv.at[to],
            device_id=near[way],
            device_id_type=MESH,
        )
        copy.start()
        started.append(copy)

    def chain(da, h):
        return da * 2 + h

    def plus(da, h):
        return 8 + da * 2 + h

    def minus(da, h):
        return 16 + da * 2 + h

    def far(da):
        send(product(da * RING + 2, 0), "b-", chain(da, 0))
        send(product(da * RING + 2, 1), "b+", chain(da, 1))

    def direct(da):
        send(product(da * RING + 3, 1), "b-", plus(da, 1))
        send(product(da * RING + 1, 0), "b+", minus(da, 0))

    def middle(da):
        send(product(da * RING + 3, 0) + landed(chain(da, 0)), "b-", plus(da, 0))
        send(product(da * RING + 1, 1) + landed(chain(da, 1)), "b+", minus(da, 1))

    def total(da, h):
        return product(da * RING, h) + landed(plus(da, h)) + landed(minus(da, h))

    far(2)
    direct(2)
    far(1)
    middle(2)
    far(3)
    direct(1)
    direct(3)
    middle(1)
    far(0)
    middle(3)
    direct(0)
    send(total(2, 0), "a-", 24)
    send(total(2, 1), "a+", 25)
    middle(0)
    send(total(1, 0), "a+", 28)
    send(total(3, 1), "a-", 27)
    send(total(3, 0) + landed(24), "a-", 26)
    send(total(1, 1) + landed(25), "a+", 29)
    for h in (0, 1):
        out[h * HALF : (h + 1) * HALF, :] = (total(0, h) + landed(26 + h) + landed(28 + h)).astype(
            BF16
        )
    for copies in sends.values():
        for copy in copies:
            copy.wait_send()
    for copy in started:
        copy.wait_send()


def per_device(loaded, lengths, offsets, gate_weight, up_weight, down_weight):
    width, hidden = gate_weight.shape
    vmem = pl.BlockSpec(memory_space=pltpu.VMEM)
    smem = pl.BlockSpec(memory_space=pltpu.SMEM)
    hbm = pl.BlockSpec(memory_space=pl.ANY)
    outgoing, table = pl.pallas_call(
        plan_kernel,
        out_shape=(
            jax.ShapeDtypeStruct((N_ROW, N_COL, CAP, WIDTH), BF16),
            jax.ShapeDtypeStruct((CAP, SRC), I32),
        ),
        in_specs=[smem, smem, vmem, vmem, vmem],
        out_specs=(vmem, vmem),
        compiler_params=pltpu.CompilerParams(vmem_limit_bytes=32 * 1024 * 1024),
        name="plan",
    )(lengths, offsets, lengths.T, offsets.T, loaded)
    arrived = lax.all_to_all(
        outgoing.reshape(SRC, CAP, WIDTH), ("row", "col"), split_axis=0, concat_axis=0, tiled=True
    ).reshape(SRC * CAP, WIDTH)
    return pl.pallas_call(
        ffn_kernel,
        out_shape=jax.ShapeDtypeStruct((TOK, WIDTH), BF16),
        in_specs=[vmem, vmem, hbm, hbm, hbm],
        out_specs=vmem,
        scratch_shapes=[
            pltpu.VMEM((width, hidden), BF16),
            pltpu.VMEM((width, hidden), BF16),
            pltpu.VMEM((hidden, width), BF16),
            pltpu.VMEM((N_COL, 2, HALF, WIDTH), BF16),
            pltpu.VMEM((TOK, hidden), F32),
            pltpu.VMEM((TOK, hidden), F32),
            pltpu.VMEM((TOK, hidden), BF16),
            pltpu.VMEM((WIDTH, SRC * CAP), BF16),
            pltpu.VMEM((30, HALF, WIDTH), BF16),
            pltpu.SemaphoreType.DMA((3,)),
            pltpu.SemaphoreType.DMA((30,)),
            pltpu.SemaphoreType.DMA((N_COL, 2)),
            pltpu.SemaphoreType.DMA((30,)),
            pltpu.SemaphoreType.DMA((30,)),
        ],
        compiler_params=pltpu.CompilerParams(
            collective_id=0, has_side_effects=True, vmem_limit_bytes=60 * 1024 * 1024
        ),
        name="ffn",
    )(arrived, table, gate_weight, up_weight, down_weight)


def solution(mesh):
    placed = (P(("row", "col"), None), P(), P(), P(None, "col"), P(None, "col"), P("col", None))
    return jax.shard_map(
        per_device, mesh=mesh, in_specs=placed, out_specs=P("row", "col"), check_vma=False
    )
```

```python
import functools

import jax
import jax.numpy as jnp
from jax import lax
from jax.experimental import pallas as pl
from jax.experimental.pallas import tpu as pltpu
from jax.sharding import PartitionSpec as P

MESH = pl.DeviceIdType.MESH
N_ROW = 8
N_COL = 16
RING = 4
LOAD = 64
CAP = 16
TRAJ = 8
TOK = 1024
HALF = 512
WIDTH = 256
SRC = N_ROW * N_COL
NT = (((1,), (1,)), ((), ()))
I32 = jnp.int32
F32 = jnp.float32
BF16 = jnp.bfloat16


def plan_kernel(len_t, off_t, loaded, arrived, table, out, local_sem, send_sem, recv_sem):
    row = lax.axis_index("row")
    col = lax.axis_index("col")
    me = row * N_COL + col
    cx = lax.div(col, RING)
    cy = lax.rem(col, RING)

    def partner(k):
        r = lax.rem(row + lax.div(k, N_COL), N_ROW)
        x = lax.rem(cx + lax.rem(lax.div(k, RING), RING), RING)
        y = lax.rem(cy + lax.rem(k, RING), RING)
        return r, x * RING + y

    barrier = pltpu.get_barrier_semaphore()

    def greet(k, carry):
        pl.semaphore_signal(barrier, inc=1, device_id=partner(k), device_id_type=MESH)
        return carry

    lax.fori_loop(1, SRC, greet, 0)
    lane = lax.broadcasted_iota(I32, (LOAD, LOAD), 1)
    sub = lax.broadcasted_iota(I32, (LOAD, LOAD), 0)
    pos_l = jnp.zeros((LOAD, LOAD), I32)
    pos_s = jnp.zeros((LOAD, LOAD), I32)
    own = lax.broadcasted_iota(I32, (TRAJ, SRC), 1) == me
    own_len = jnp.sum(jnp.where(own, len_t[...], 0).astype(F32), axis=1, keepdims=True).astype(I32)
    own_off = jnp.sum(jnp.where(own, off_t[...], 0).astype(F32), axis=1, keepdims=True).astype(I32)
    start = jnp.zeros((1, 1), I32)
    for j in range(TRAJ):
        end = start + own_len[j : j + 1, :]
        shift = own_off[j : j + 1, :] - start
        pos_l = jnp.where((lane >= start) & (lane < end), shift + lane, pos_l)
        pos_s = jnp.where((sub >= start) & (sub < end), shift + sub, pos_s)
        start = end
    block_l = pos_l // TOK
    block_s = pos_s // TOK
    rank = jnp.sum(
        jnp.where((block_l == block_s) & (sub < lane), 1.0, 0.0), axis=0, keepdims=True
    ).astype(I32)
    target = block_l[0:1, :] * CAP + rank
    slot = lax.broadcasted_iota(I32, (N_ROW * CAP, LOAD), 0)
    select = jnp.where(target == slot, 1.0, 0.0).astype(BF16)
    for c in range(N_COL):
        picked = jnp.dot(select, loaded[:, c * WIDTH : (c + 1) * WIDTH], preferred_element_type=F32)
        out[:, c] = picked.astype(BF16).reshape(N_ROW, CAP, WIDTH)
    pl.semaphore_wait(barrier, SRC - 1)

    def copy_to(k):
        r, c = partner(k)
        return pltpu.make_async_remote_copy(
            src_ref=out.at[r, c],
            dst_ref=arrived.at[me],
            send_sem=send_sem,
            recv_sem=recv_sem,
            device_id=(r, c),
            device_id_type=MESH,
        )

    def start(k, carry):
        copy_to(k).start()
        return carry

    lax.fori_loop(1, SRC, start, 0)
    own_copy = pltpu.make_async_copy(out.at[row, col], arrived.at[me], local_sem)
    own_copy.start()

    tok = lax.broadcasted_iota(I32, (LOAD, SRC), 0)
    pos = jnp.zeros((LOAD, SRC), I32)
    start = jnp.zeros((1, SRC), I32)
    for j in range(TRAJ):
        end = start + len_t[j : j + 1, :]
        pos = jnp.where((tok >= start) & (tok < end), off_t[j : j + 1, :] - start + tok, pos)
        start = end
    mine = pos // TOK == row
    below = jnp.where(sub > lane, 1.0, 0.0).astype(BF16)
    order = jnp.dot(below, jnp.where(mine, 1.0, 0.0).astype(BF16), preferred_element_type=F32)
    order = order.astype(I32)
    in_row = jnp.where(mine, pos % TOK + 1, 0)
    by_slot = jnp.concatenate(
        [
            jnp.sum(jnp.where(order == q, in_row, 0).astype(F32), axis=0, keepdims=True)
            for q in range(CAP)
        ],
        axis=0,
    ).astype(I32)
    wide_s = lax.broadcasted_iota(I32, (SRC, CAP), 0)
    wide_l = lax.broadcasted_iota(I32, (SRC, CAP), 1)
    spread = jnp.where(wide_s % CAP == wide_l, 1.0, 0.0).astype(BF16)
    sq_s = lax.broadcasted_iota(I32, (SRC, SRC), 0)
    sq_l = lax.broadcasted_iota(I32, (SRC, SRC), 1)
    keep = sq_l % 8 == sq_s // CAP
    group_s = lax.broadcasted_iota(I32, (CAP, SRC), 0)
    group_l = lax.broadcasted_iota(I32, (CAP, SRC), 1)
    group = jnp.where(group_l // 8 == group_s, 1.0, 0.0).astype(BF16)
    total = jnp.zeros((CAP, SRC), F32)
    for part, scale in ((by_slot // 32, 32.0), (by_slot % 32, 1.0)):
        y = jnp.dot(spread, part.astype(F32).astype(BF16), preferred_element_type=F32)
        y = jnp.where(keep, y, 0.0).astype(BF16)
        total = total + scale * lax.dot_general(
            group, y, (((1,), (1,)), ((), ())), preferred_element_type=F32
        )
    table[...] = total.astype(I32) - 1
    own_copy.wait()
    others = arrived.at[pl.ds(0, SRC - 1)]
    pltpu.make_async_copy(others, others, recv_sem).wait()
    pltpu.make_async_copy(others, others, send_sem).wait()


def ffn_kernel(
    arrived, table, wg_hbm, wu_hbm, wd_hbm, out,
    wg, wu, wd, x, accg, accu, hid, hot, got,
    w_sem, ag_send, ag_recv, rs_send, rs_recv,
):
    row = lax.axis_index("row")
    col = lax.axis_index("col")
    swap = lax.rem(row, 2)
    cx = lax.div(col, RING)
    cy = lax.rem(col, RING)
    a0 = (1 - swap) * cx + swap * cy
    b0 = (1 - swap) * cy + swap * cx

    def col_of(da, db):
        a = lax.rem(a0 + da, RING)
        b = lax.rem(b0 + db, RING)
        return (1 - swap) * (a * RING + b) + swap * (b * RING + a)

    near = {
        "a+": (row, col_of(1, 0)),
        "a-": (row, col_of(3, 0)),
        "b+": (row, col_of(0, 1)),
        "b-": (row, col_of(0, 3)),
    }
    loads = [
        pltpu.make_async_copy(src, dst, w_sem.at[i])
        for i, (src, dst) in enumerate(((wg_hbm, wg), (wu_hbm, wu), (wd_hbm, wd)))
    ]
    for load in loads:
        load.start()

    barrier = pltpu.get_barrier_semaphore()
    for who in near.values():
        pl.semaphore_signal(barrier, inc=1, device_id=who, device_id_type=MESH)

    def compact(m):
        place = lax.broadcasted_iota(I32, (WIDTH, SRC), 0) + m * WIDTH
        for g in range(CAP):
            hot[:, g * SRC : (g + 1) * SRC] = jnp.where(
                table[g : g + 1, :] == place, 1.0, 0.0
            ).astype(BF16)
        x[0, m // 2, (m % 2) * WIDTH : (m % 2 + 1) * WIDTH, :] = jnp.dot(
            hot[...], arrived[...], preferred_element_type=F32
        ).astype(BF16)

    sends = {}
    count = [0]

    def forward(slot, h, way, to):
        copy = pltpu.make_async_remote_copy(
            src_ref=x.at[slot, h],
            dst_ref=x.at[to, h],
            send_sem=ag_send.at[count[0]],
            recv_sem=ag_recv.at[to, h],
            device_id=near[way],
            device_id_type=MESH,
        )
        count[0] += 1
        copy.start()
        sends.setdefault((slot, h), []).append(copy)

    def pass_on(slot, h):
        da, db = slot // RING, slot % RING
        if db == 0:
            if da == 0:
                forward(slot, h, "a-", 1 * RING)
                forward(slot, h, "a+", 3 * RING)
            if da == 3 and h == 0:
                forward(slot, h, "a+", 2 * RING)
            if da == 1 and h == 1:
                forward(slot, h, "a-", 2 * RING)
            forward(slot, h, "b-", da * RING + 1)
            forward(slot, h, "b+", da * RING + 3)
        if db == 3 and h == 0:
            forward(slot, h, "b+", da * RING + 2)
        if db == 1 and h == 1:
            forward(slot, h, "b-", da * RING + 2)

    def take(slot, h):
        pltpu.make_async_copy(x.at[slot, h], x.at[slot, h], ag_recv.at[slot, h]).wait()
        pass_on(slot, h)

    def gate_up(slots, first=False, last=False):
        ks = [
            pl.ds(pl.multiple_of(col_of(s // RING, s % RING) * WIDTH, WIDTH), WIDTH) for s in slots
        ]

        def chunk(m, carry):
            h = lax.div(m, 2)
            src = pl.ds(pl.multiple_of(lax.rem(m, 2) * WIDTH, WIDTH), WIDTH)
            dst = pl.ds(pl.multiple_of(m * WIDTH, WIDTH), WIDTH)
            g = u = None
            for s, k in zip(slots, ks):
                lhs = x[s, h, src, :]
                dg = lax.dot_general(lhs, wg[:, k], NT, preferred_element_type=F32)
                du = lax.dot_general(lhs, wu[:, k], NT, preferred_element_type=F32)
                g = dg if g is None else g + dg
                u = du if u is None else u + du
            if not first:
                g = accg[dst, :] + g
                u = accu[dst, :] + u
            if last:
                hid[dst, :] = (g / (1.0 + jnp.exp(-g)) * u).astype(BF16)
            else:
                accg[dst, :] = g
                accu[dst, :] = u
            return carry

        lax.fori_loop(0, TOK // WIDTH, chunk, 0)

    compact(0)
    compact(1)
    pl.semaphore_wait(barrier, 4)
    pass_on(0, 0)
    compact(2)
    compact(3)
    pass_on(0, 1)
    groups = [[4, 12], [1, 3], [8, 2], [5, 7], [13, 15], [6, 14], [9, 11], [10]]
    for load in loads[:2]:
        load.wait()
    pending = [0]
    for i, group in enumerate(groups):
        for slot in group:
            take(slot, 0)
            take(slot, 1)
        gate_up(pending, first=i == 0)
        pending = group
    gate_up(pending, last=True)
    loads[2].wait()

    spots = [(s, h) for s in (2, 6, 14, 10, 0, 1, 3, 4, 12, 5, 7, 13, 15, 8, 9, 11) for h in (0, 1)]
    started = []

    def product(slot, h):
        cols = pl.ds(pl.multiple_of(col_of(slot // RING, slot % RING) * WIDTH, WIDTH), WIDTH)
        return jnp.dot(
            hid[h * HALF : (h + 1) * HALF, :], wd[:, cols], preferred_element_type=F32
        )

    def landed(i):
        pltpu.make_async_copy(got.at[i], got.at[i], rs_recv.at[i]).wait()
        return got[i].astype(F32)

    def send(value, way, to):
        n = len(started)
        spot = spots[n]
        for copy in sends.pop(spot, []):
            copy.wait_send()
        x[spot[0], spot[1]] = value.astype(BF16)
        copy = pltpu.make_async_remote_copy(
            src_ref=x.at[spot[0], spot[1]],
            dst_ref=got.at[to],
            send_sem=rs_send.at[n],
            recv_sem=rs_recv.at[to],
            device_id=near[way],
            device_id_type=MESH,
        )
        copy.start()
        started.append(copy)

    def chain(da, h):
        return da * 2 + h

    def plus(da, h):
        return 8 + da * 2 + h

    def minus(da, h):
        return 16 + da * 2 + h

    def far(da):
        send(product(da * RING + 2, 0), "b-", chain(da, 0))
        send(product(da * RING + 2, 1), "b+", chain(da, 1))

    def direct(da):
        send(product(da * RING + 3, 1), "b-", plus(da, 1))
        send(product(da * RING + 1, 0), "b+", minus(da, 0))

    def middle(da):
        send(product(da * RING + 3, 0) + landed(chain(da, 0)), "b-", plus(da, 0))
        send(product(da * RING + 1, 1) + landed(chain(da, 1)), "b+", minus(da, 1))

    def total(da, h):
        return product(da * RING, h) + landed(plus(da, h)) + landed(minus(da, h))

    far(2)
    direct(2)
    far(1)
    middle(2)
    far(3)
    direct(1)
    direct(3)
    middle(1)
    far(0)
    middle(3)
    direct(0)
    send(total(2, 0), "a-", 24)
    send(total(2, 1), "a+", 25)
    middle(0)
    send(total(1, 0), "a+", 28)
    send(total(3, 1), "a-", 27)
    send(total(3, 0) + landed(24), "a-", 26)
    send(total(1, 1) + landed(25), "a+", 29)
    for h in (0, 1):
        out[h * HALF : (h + 1) * HALF, :] = (total(0, h) + landed(26 + h) + landed(28 + h)).astype(
            BF16
        )
    for copies in sends.values():
        for copy in copies:
            copy.wait_send()
    for copy in started:
        copy.wait_send()


def per_device(loaded, lengths, offsets, gate_weight, up_weight, down_weight):
    width, hidden = gate_weight.shape
    vmem = pl.BlockSpec(memory_space=pltpu.VMEM)
    hbm = pl.BlockSpec(memory_space=pl.ANY)
    arrived, table = pl.pallas_call(
        plan_kernel,
        out_shape=(
            jax.ShapeDtypeStruct((SRC, CAP, WIDTH), BF16),
            jax.ShapeDtypeStruct((CAP, SRC), I32),
        ),
        in_specs=[vmem, vmem, vmem],
        out_specs=(vmem, vmem),
        scratch_shapes=[
            pltpu.VMEM((N_ROW, N_COL, CAP, WIDTH), BF16),
            pltpu.SemaphoreType.DMA,
            pltpu.SemaphoreType.DMA,
            pltpu.SemaphoreType.DMA,
        ],
        compiler_params=pltpu.CompilerParams(
            collective_id=1, has_side_effects=True, vmem_limit_bytes=32 * 1024 * 1024
        ),
        name="dispatch",
    )(lengths.T, offsets.T, loaded)
    return pl.pallas_call(
        ffn_kernel,
        out_shape=jax.ShapeDtypeStruct((TOK, WIDTH), BF16),
        in_specs=[vmem, vmem, hbm, hbm, hbm],
        out_specs=vmem,
        scratch_shapes=[
            pltpu.VMEM((hidden, width), BF16),
            pltpu.VMEM((hidden, width), BF16),
            pltpu.VMEM((hidden, width), BF16),
            pltpu.VMEM((N_COL, 2, HALF, WIDTH), BF16),
            pltpu.VMEM((TOK, hidden), F32),
            pltpu.VMEM((TOK, hidden), F32),
            pltpu.VMEM((TOK, hidden), BF16),
            pltpu.VMEM((WIDTH, SRC * CAP), BF16),
            pltpu.VMEM((30, HALF, WIDTH), BF16),
            pltpu.SemaphoreType.DMA((3,)),
            pltpu.SemaphoreType.DMA((30,)),
            pltpu.SemaphoreType.DMA((N_COL, 2)),
            pltpu.SemaphoreType.DMA((30,)),
            pltpu.SemaphoreType.DMA((30,)),
        ],
        compiler_params=pltpu.CompilerParams(
            collective_id=0, has_side_effects=True, vmem_limit_bytes=60 * 1024 * 1024
        ),
        name="ffn",
    )(arrived.reshape(SRC * CAP, WIDTH), table, gate_weight.T, up_weight.T, down_weight)


def solution(mesh):
    placed = (P(("row", "col"), None), P(), P(), P(None, "col"), P(None, "col"), P("col", None))
    return jax.shard_map(
        per_device, mesh=mesh, in_specs=placed, out_specs=P("row", "col"), check_vma=False
    )
```

```python
import functools

import jax
import jax.numpy as jnp
from jax import lax
from jax.experimental import pallas as pl
from jax.experimental.pallas import tpu as pltpu
from jax.sharding import PartitionSpec as P

MESH = pl.DeviceIdType.MESH
N_ROW = 8
N_COL = 16
RING = 4
LOAD = 64
CAP = 16
TRAJ = 8
TOK = 1024
HALF = 512
WIDTH = 256
PIECE = 256
SRC = N_ROW * N_COL
NT = (((1,), (1,)), ((), ()))
I32 = jnp.int32
F32 = jnp.float32
BF16 = jnp.bfloat16
GROUPS = ((0,), (4, 12), (1, 3), (8, 2), (5, 7), (13, 15), (6, 14), (9, 11), (10,))
PROGRAM = (
    (0, 1), (1, 1), (0, 0), (0, 3), (1, 0), (1, 3), (3, 4, 1), (2, 0), (3, 12, 0), (3, 4, 0), (3, 7, 1), (2, 1),
    (3, 12, 1), (4, 0, 1), (3, 8, 1), (3, 7, 0), (3, 5, 1), (0, 2), (3, 8, 0), (3, 13, 1), (3, 1, 0),
    (3, 15, 0), (3, 11, 1), (3, 15, 1), (3, 13, 0), (3, 5, 0), (1, 2), (4, 0, 5), (3, 3, 0), (2, 3), (3, 1, 1),
    (4, 0, 4), (3, 9, 0), (4, 0, 0), (3, 11, 0), (3, 9, 1), (3, 3, 1), (3, 6, 0), (3, 14, 1), (4, 0, 7),
    (3, 14, 0), (2, 2), (3, 6, 1), (3, 4, 3), (4, 0, 2), (3, 2, 1), (3, 12, 2), (3, 1, 3), (3, 2, 0), (4, 0, 3),
    (3, 10, 0), (4, 0, 6), (3, 4, 2), (3, 10, 1), (3, 12, 3), (4, 0, 8), (5, 0, 0, 3, 0), (3, 3, 2), (4, 1, 0),
    (5, 0, 0, 0, 0), (5, 0, 0, 1, 1), (3, 7, 3), (5, 0, 0, 2, 0), (3, 1, 2), (3, 15, 2), (4, 1, 1), (3, 3, 3),
    (3, 5, 3), (3, 7, 2), (3, 15, 3), (3, 8, 2), (4, 1, 2), (5, 0, 0, 1, 0), (5, 0, 0, 3, 1), (3, 13, 2),
    (5, 0, 0, 2, 1), (3, 8, 3), (3, 2, 2), (3, 2, 3), (3, 5, 2), (4, 1, 4), (3, 13, 3), (4, 1, 3), (4, 1, 5),
    (3, 11, 2), (5, 0, 1, 0, 1), (3, 6, 2), (5, 0, 1, 3, 0), (5, 0, 2, 1, 1), (5, 0, 0, 0, 1), (5, 0, 2, 2, 0),
    (5, 0, 2, 2, 1), (5, 0, 1, 2, 0), (3, 9, 2), (3, 14, 2), (5, 0, 2, 3, 1), (3, 11, 3), (5, 0, 1, 1, 0),
    (3, 9, 3), (5, 0, 1, 1, 1), (4, 1, 7), (3, 10, 2), (5, 0, 2, 0, 0), (5, 0, 1, 0, 0), (3, 14, 3),
    (5, 0, 2, 3, 0), (3, 6, 3), (4, 1, 6), (3, 10, 3), (5, 0, 1, 3, 1), (5, 0, 1, 2, 1), (4, 1, 8),
    (5, 1, 0, 0, 0), (5, 1, 0, 2, 1), (5, 1, 0, 1, 1), (5, 1, 0, 2, 0), (5, 1, 0, 0, 1), (5, 1, 0, 3, 0),
    (5, 1, 1, 1, 0), (5, 1, 1, 1, 1), (5, 1, 0, 3, 1), (5, 0, 3, 0, 1), (5, 1, 1, 0, 1), (5, 0, 2, 1, 0),
    (5, 1, 0, 1, 0), (5, 1, 1, 2, 0), (5, 1, 2, 2, 0), (5, 1, 2, 1, 1), (5, 1, 2, 0, 0), (5, 1, 2, 2, 1),
    (5, 1, 1, 2, 1), (5, 1, 2, 3, 1), (5, 1, 1, 3, 1), (5, 1, 1, 0, 0), (5, 0, 5, 0, 1), (5, 1, 2, 1, 0),
    (5, 0, 3, 0, 0), (5, 1, 3, 0, 0), (5, 1, 1, 3, 0), (5, 1, 2, 3, 0), (5, 0, 4, 0, 0), (5, 1, 3, 0, 1),
    (5, 1, 4, 0, 1), (5, 0, 2, 0, 1), (5, 0, 4, 0, 1), (5, 1, 4, 0, 0), (5, 1, 2, 0, 1), (5, 0, 5, 0, 0),
    (5, 1, 5, 0, 0), (5, 1, 5, 0, 1), (6, 0, 0), (6, 0, 1), (6, 1, 0), (6, 1, 1),
)


def layer_kernel(
    len_hbm, off_hbm, loaded_hbm, wg_hbm, wu_hbm, wd_hbm, out,
    len_t, off_t, loaded, outgoing, arrived, table, hot, wg, wu, wd, x, accg, accu, hid, got,
    in_sem, w_sem, own_sem, spread_send, spread_recv, ag_send, ag_recv, rs_send, rs_recv,
):
    row = lax.axis_index("row")
    col = lax.axis_index("col")
    me = row * N_COL + col
    cx = lax.div(col, RING)
    cy = lax.rem(col, RING)

    inputs = [
        pltpu.make_async_copy(src, dst, in_sem.at[i])
        for i, (src, dst) in enumerate(
            ((len_hbm, len_t), (off_hbm, off_t), (loaded_hbm, loaded))
        )
    ]
    loads = [
        pltpu.make_async_copy(src, dst, w_sem.at[i])
        for i, (src, dst) in enumerate(((wg_hbm, wg), (wu_hbm, wu), (wd_hbm, wd)))
    ]
    for copy in inputs:
        copy.start()

    def partner(k):
        r = lax.rem(row + lax.div(k, N_COL), N_ROW)
        a = lax.rem(cx + lax.rem(lax.div(k, RING), RING), RING)
        b = lax.rem(cy + lax.rem(k, RING), RING)
        return r, a * RING + b

    barrier = pltpu.get_barrier_semaphore()

    def greet(k, carry):
        pl.semaphore_signal(barrier, inc=1, device_id=partner(k), device_id_type=MESH)
        return carry

    lax.fori_loop(1, SRC, greet, 0)

    for copy in inputs:
        copy.wait()
    for load in loads:
        load.start()
    lane = lax.broadcasted_iota(I32, (LOAD, LOAD), 1)
    sub = lax.broadcasted_iota(I32, (LOAD, LOAD), 0)
    pos_l = jnp.zeros((LOAD, LOAD), I32)
    pos_s = jnp.zeros((LOAD, LOAD), I32)
    own = lax.broadcasted_iota(I32, (TRAJ, SRC), 1) == me
    own_len = jnp.sum(jnp.where(own, len_t[...], 0).astype(F32), axis=1, keepdims=True).astype(I32)
    own_off = jnp.sum(jnp.where(own, off_t[...], 0).astype(F32), axis=1, keepdims=True).astype(I32)
    start = jnp.zeros((1, 1), I32)
    for j in range(TRAJ):
        end = start + own_len[j : j + 1, :]
        shift = own_off[j : j + 1, :] - start
        pos_l = jnp.where((lane >= start) & (lane < end), shift + lane, pos_l)
        pos_s = jnp.where((sub >= start) & (sub < end), shift + sub, pos_s)
        start = end
    block_l = pos_l // TOK
    block_s = pos_s // TOK
    rank = jnp.sum(
        jnp.where((block_l == block_s) & (sub < lane), 1.0, 0.0), axis=0, keepdims=True
    ).astype(I32)
    target = block_l[0:1, :] * CAP + rank
    slot = lax.broadcasted_iota(I32, (N_ROW * CAP, LOAD), 0)
    select = jnp.where(target == slot, 1.0, 0.0).astype(BF16)
    for c in range(N_COL):
        picked = jnp.dot(select, loaded[:, c * WIDTH : (c + 1) * WIDTH], preferred_element_type=F32)
        outgoing[:, c] = picked.astype(BF16).reshape(N_ROW, CAP, WIDTH)
    pl.semaphore_wait(barrier, SRC - 1)

    def spread(k, carry):
        r, c = partner(k)
        pltpu.make_async_remote_copy(
            src_ref=outgoing.at[r, c],
            dst_ref=arrived.at[me],
            send_sem=spread_send,
            recv_sem=spread_recv,
            device_id=(r, c),
            device_id_type=MESH,
        ).start()
        return carry

    lax.fori_loop(1, SRC, spread, 0)
    own_copy = pltpu.make_async_copy(outgoing.at[row, col], arrived.at[me], own_sem)
    own_copy.start()

    tok = lax.broadcasted_iota(I32, (LOAD, SRC), 0)
    pos = jnp.zeros((LOAD, SRC), I32)
    start = jnp.zeros((1, SRC), I32)
    for j in range(TRAJ):
        end = start + len_t[j : j + 1, :]
        pos = jnp.where((tok >= start) & (tok < end), off_t[j : j + 1, :] - start + tok, pos)
        start = end
    mine = pos // TOK == row
    below = jnp.where(sub > lane, 1.0, 0.0).astype(BF16)
    order = jnp.dot(below, jnp.where(mine, 1.0, 0.0).astype(BF16), preferred_element_type=F32)
    order = order.astype(I32)
    in_row = jnp.where(mine, pos % TOK + 1, 0)
    by_slot = jnp.concatenate(
        [
            jnp.sum(jnp.where(order == q, in_row, 0).astype(F32), axis=0, keepdims=True)
            for q in range(CAP)
        ],
        axis=0,
    ).astype(I32)
    wide_s = lax.broadcasted_iota(I32, (SRC, CAP), 0)
    wide_l = lax.broadcasted_iota(I32, (SRC, CAP), 1)
    spread = jnp.where(wide_s % CAP == wide_l, 1.0, 0.0).astype(BF16)
    sq_s = lax.broadcasted_iota(I32, (SRC, SRC), 0)
    sq_l = lax.broadcasted_iota(I32, (SRC, SRC), 1)
    keep = sq_l % 8 == sq_s // CAP
    group_s = lax.broadcasted_iota(I32, (CAP, SRC), 0)
    group_l = lax.broadcasted_iota(I32, (CAP, SRC), 1)
    group = jnp.where(group_l // 8 == group_s, 1.0, 0.0).astype(BF16)
    total = jnp.zeros((CAP, SRC), F32)
    for part, scale in ((by_slot // 32, 32.0), (by_slot % 32, 1.0)):
        y = jnp.dot(spread, part.astype(F32).astype(BF16), preferred_element_type=F32)
        y = jnp.where(keep, y, 0.0).astype(BF16)
        total = total + scale * lax.dot_general(
            group, y, (((1,), (1,)), ((), ())), preferred_element_type=F32
        )
    table[...] = total.astype(I32) - 1

    def place(m, carry):
        first = pl.multiple_of(m * PIECE, PIECE)
        at = lax.broadcasted_iota(I32, (PIECE, SRC), 0) + first
        for g in range(CAP):
            hot[pl.ds(first, PIECE), g * SRC : (g + 1) * SRC] = jnp.where(
                table[g : g + 1, :] == at, 1.0, 0.0
            ).astype(BF16)
        return carry

    lax.fori_loop(0, TOK // PIECE, place, 0)

    swap = lax.rem(row, 2)
    a0 = (1 - swap) * cx + swap * cy
    b0 = (1 - swap) * cy + swap * cx

    def col_of(da, db):
        a = lax.rem(a0 + da, RING)
        b = lax.rem(b0 + db, RING)
        return (1 - swap) * (a * RING + b) + swap * (b * RING + a)

    near = {
        "a+": (row, col_of(1, 0)),
        "a-": (row, col_of(3, 0)),
        "b+": (row, col_of(0, 1)),
        "b-": (row, col_of(0, 3)),
    }
    own_copy.wait()
    others = arrived.at[pl.ds(0, SRC - 1)]
    pltpu.make_async_copy(others, others, spread_recv).wait()

    def compact(m):
        x[0, m] = jnp.dot(
            hot[m * PIECE : (m + 1) * PIECE, :],
            arrived[...].reshape(SRC * CAP, WIDTH),
            preferred_element_type=F32,
        ).astype(BF16)

    sends = {}
    count = [0]

    def forward(slot, m, way, to):
        copy = pltpu.make_async_remote_copy(
            src_ref=x.at[slot, m],
            dst_ref=x.at[to, m],
            send_sem=ag_send.at[count[0]],
            recv_sem=ag_recv.at[to, m],
            device_id=near[way],
            device_id_type=MESH,
        )
        count[0] += 1
        copy.start()
        sends.setdefault((slot, m), []).append(copy)

    def own_first(m):
        forward(0, m, "a-", 1 * RING)
        forward(0, m, "a+", 3 * RING)

    def own_second(m):
        forward(0, m, "b-", 1)
        forward(0, m, "b+", 3)

    def take(slot, m):
        pltpu.make_async_copy(x.at[slot, m], x.at[slot, m], ag_recv.at[slot, m]).wait()
        da, db, q = slot // RING, slot % RING, m % 2
        if db == 0:
            if da == 3 and q == 0:
                forward(slot, m, "a+", 2 * RING)
            if da == 1 and q == 1:
                forward(slot, m, "a-", 2 * RING)
            forward(slot, m, "b-", da * RING + 1)
            forward(slot, m, "b+", da * RING + 3)
        if db == 3 and q == 0:
            forward(slot, m, "b+", da * RING + 2)
        if db == 1 and q == 1:
            forward(slot, m, "b-", da * RING + 2)

    done = [0, 0]

    def gate_up(t, group):
        if sum(done) == 0:
            for load in loads[:2]:
                load.wait()
        slots = GROUPS[group]
        first, last = done[t] == 0, done[t] == len(GROUPS) - 1
        done[t] += 1
        ks = [
            pl.ds(pl.multiple_of(col_of(s // RING, s % RING) * WIDTH, WIDTH), WIDTH) for s in slots
        ]
        g = u = None
        for s, k in zip(slots, ks):
            lhs = x[s, 2 * t : 2 * t + 2].reshape(HALF, WIDTH)
            dg = lax.dot_general(lhs, wg[:, k], NT, preferred_element_type=F32)
            du = lax.dot_general(lhs, wu[:, k], NT, preferred_element_type=F32)
            g = dg if g is None else g + dg
            u = du if u is None else u + du
        if not first:
            g = accg[...] + g
            u = accu[...] + u
        if last:
            hid[t * HALF : (t + 1) * HALF, :] = (g / (1.0 + jnp.exp(-g)) * u).astype(BF16)
        else:
            accg[...] = g
            accu[...] = u

    order = [2, 6, 14, 10, 0, 1, 3, 4, 12, 5, 7, 13, 15, 8, 9, 11]
    spots = [[(s, 2 * t + q) for s in order for q in (0, 1)] for t in (0, 1)]
    started = []

    def product(slot, m):
        cols = pl.ds(pl.multiple_of(col_of(slot // RING, slot % RING) * WIDTH, WIDTH), WIDTH)
        return jnp.dot(
            hid[m * PIECE : (m + 1) * PIECE, :], wd[:, cols], preferred_element_type=F32
        )

    def landed(i, t):
        i = t * 30 + i
        pltpu.make_async_copy(got.at[i], got.at[i], rs_recv.at[i]).wait()
        return got[i].astype(F32)

    def send(value, way, to, t):
        n = len(started)
        spot = spots[t].pop(0)
        for copy in sends.pop(spot, []):
            copy.wait_send()
        x[spot[0], spot[1]] = value.astype(BF16)
        to = t * 30 + to
        copy = pltpu.make_async_remote_copy(
            src_ref=x.at[spot[0], spot[1]],
            dst_ref=got.at[to],
            send_sem=rs_send.at[n],
            recv_sem=rs_recv.at[to],
            device_id=near[way],
            device_id_type=MESH,
        )
        copy.start()
        started.append(copy)

    def chain(da, q):
        return da * 2 + q

    def plus(da, q):
        return 8 + da * 2 + q

    def minus(da, q):
        return 16 + da * 2 + q

    def scatter(t, kind, da, q):
        if kind == 0:
            send(product(da * RING + 2, 2 * t + q), "b+" if q else "b-", chain(da, q), t)
        elif kind == 1:
            if q:
                send(product(da * RING + 3, 2 * t + 1), "b-", plus(da, 1), t)
            else:
                send(product(da * RING + 1, 2 * t), "b+", minus(da, 0), t)
        elif kind == 2:
            if q:
                value = product(da * RING + 1, 2 * t + 1) + landed(chain(da, 1), t)
                send(value, "b+", minus(da, 1), t)
            else:
                value = product(da * RING + 3, 2 * t) + landed(chain(da, 0), t)
                send(value, "b-", plus(da, 0), t)
        elif kind == 3:
            send(total(t, 2, q), "a+" if q else "a-", 24 + q, t)
        elif kind == 4:
            if q:
                send(total(t, 3, 1), "a-", 27, t)
            else:
                send(total(t, 1, 0), "a+", 28, t)
        elif q:
            send(total(t, 1, 1) + landed(25, t), "a+", 29, t)
        else:
            send(total(t, 3, 0) + landed(24, t), "a-", 26, t)

    def total(t, da, q):
        return product(da * RING, 2 * t + q) + landed(plus(da, q), t) + landed(minus(da, q), t)

    def finish(t, q):
        m = 2 * t + q
        value = total(t, 0, q) + landed(26 + q, t) + landed(28 + q, t)
        out[m * PIECE : (m + 1) * PIECE, :] = value.astype(BF16)

    steps = (compact, own_first, own_second, take, gate_up, scatter, finish)
    for what, *which in PROGRAM:
        if what == 5 and not started:
            loads[2].wait()
        steps[what](*which)
    for copies in sends.values():
        for copy in copies:
            copy.wait_send()
    for copy in started:
        copy.wait_send()
    pltpu.make_async_copy(others, others, spread_send).wait()


def per_device(loaded, lengths, offsets, gate_weight, up_weight, down_weight):
    width, hidden = gate_weight.shape
    hbm = pl.BlockSpec(memory_space=pl.ANY)
    return pl.pallas_call(
        layer_kernel,
        out_shape=jax.ShapeDtypeStruct((TOK, WIDTH), BF16),
        in_specs=[hbm] * 6,
        out_specs=pl.BlockSpec(memory_space=pltpu.VMEM),
        scratch_shapes=[
            pltpu.VMEM((TRAJ, SRC), I32),
            pltpu.VMEM((TRAJ, SRC), I32),
            pltpu.VMEM((LOAD, width), BF16),
            pltpu.VMEM((N_ROW, N_COL, CAP, WIDTH), BF16),
            pltpu.VMEM((SRC, CAP, WIDTH), BF16),
            pltpu.VMEM((CAP, SRC), I32),
            pltpu.VMEM((TOK, SRC * CAP), BF16),
            pltpu.VMEM((hidden, width), BF16),
            pltpu.VMEM((hidden, width), BF16),
            pltpu.VMEM((hidden, width), BF16),
            pltpu.VMEM((N_COL, 4, PIECE, WIDTH), BF16),
            pltpu.VMEM((HALF, hidden), F32),
            pltpu.VMEM((HALF, hidden), F32),
            pltpu.VMEM((TOK, hidden), BF16),
            pltpu.VMEM((60, PIECE, WIDTH), BF16),
            pltpu.SemaphoreType.DMA((3,)),
            pltpu.SemaphoreType.DMA((3,)),
            pltpu.SemaphoreType.DMA,
            pltpu.SemaphoreType.DMA,
            pltpu.SemaphoreType.DMA,
            pltpu.SemaphoreType.DMA((60,)),
            pltpu.SemaphoreType.DMA((N_COL, 4)),
            pltpu.SemaphoreType.DMA((60,)),
            pltpu.SemaphoreType.DMA((60,)),
        ],
        compiler_params=pltpu.CompilerParams(
            collective_id=0, has_side_effects=True, vmem_limit_bytes=60 * 1024 * 1024
        ),
        name="layer",
    )(lengths.T, offsets.T, loaded, gate_weight.T, up_weight.T, down_weight)


def solution(mesh):
    placed = (P(("row", "col"), None), P(), P(), P(None, "col"), P(None, "col"), P("col", None))
    return jax.shard_map(
        per_device, mesh=mesh, in_specs=placed, out_specs=P("row", "col"), check_vma=False
    )
```

```python
import functools

import jax
import jax.numpy as jnp
from jax import lax
from jax.experimental import pallas as pl
from jax.experimental.pallas import tpu as pltpu
from jax.sharding import PartitionSpec as P

MESH = pl.DeviceIdType.MESH
N_ROW = 8
N_COL = 16
RING = 4
LOAD = 64
CAP = 16
TRAJ = 8
TOK = 1024
HALF = 512
WIDTH = 256
PIECE = 256
SRC = N_ROW * N_COL
NT = (((1,), (1,)), ((), ()))
I32 = jnp.int32
F32 = jnp.float32
BF16 = jnp.bfloat16
GROUPS = ((0,), (4, 12), (1, 3), (8, 2), (5, 7), (13, 15), (6, 14), (9, 11), (10,))
PROGRAM = (
    (0, 1), (1, 1), (0, 0), (0, 3), (2, 0), (1, 0), (3, 4, 1), (0, 2), (4, 0, 0), (2, 1), (3, 1, 0), (3, 12, 0),
    (3, 7, 1), (3, 4, 0), (3, 5, 1), (3, 12, 1), (3, 8, 1), (3, 8, 0), (3, 13, 0), (4, 0, 1), (3, 15, 0),
    (3, 11, 1), (3, 7, 0), (1, 2), (3, 13, 1), (3, 9, 1), (1, 3), (3, 11, 0), (3, 3, 0), (3, 3, 1), (3, 9, 0),
    (3, 1, 1), (4, 0, 2), (3, 15, 1), (3, 5, 0), (4, 0, 7), (2, 3), (2, 2), (4, 0, 4), (4, 0, 5), (3, 6, 1),
    (3, 4, 3), (3, 6, 0), (3, 14, 0), (3, 10, 1), (3, 14, 1), (4, 0, 6), (3, 12, 2), (3, 10, 0), (3, 12, 3),
    (3, 2, 1), (3, 4, 2), (3, 2, 0), (4, 0, 8), (4, 0, 3), (5, 0, 0, 2, 1), (5, 0, 0, 0, 0), (3, 5, 3),
    (3, 1, 2), (3, 1, 3), (5, 0, 0, 1, 1), (4, 1, 1), (5, 0, 0, 2, 0), (3, 8, 3), (3, 8, 2), (3, 3, 2),
    (3, 5, 2), (5, 0, 0, 1, 0), (3, 7, 3), (4, 1, 0), (3, 3, 3), (5, 0, 0, 0, 1), (4, 1, 2), (3, 13, 2),
    (3, 13, 3), (5, 0, 2, 2, 1), (3, 15, 2), (3, 7, 2), (4, 1, 4), (3, 15, 3), (5, 0, 0, 3, 1), (4, 1, 5),
    (3, 11, 3), (5, 0, 0, 3, 0), (3, 6, 3), (3, 11, 2), (5, 0, 1, 2, 0), (3, 2, 2), (5, 0, 1, 2, 1),
    (5, 0, 1, 3, 1), (3, 14, 3), (3, 9, 2), (3, 2, 3), (5, 0, 2, 1, 0), (3, 9, 3), (4, 1, 7), (5, 0, 1, 3, 0),
    (5, 0, 1, 1, 0), (5, 0, 2, 0, 0), (5, 0, 1, 0, 0), (3, 6, 2), (5, 0, 1, 1, 1), (5, 0, 1, 0, 1), (3, 14, 2),
    (5, 0, 2, 3, 1), (5, 0, 2, 3, 0), (4, 1, 6), (5, 0, 2, 1, 1), (3, 10, 2), (5, 0, 3, 0, 1), (4, 1, 3),
    (3, 10, 3), (5, 0, 2, 2, 0), (4, 1, 8), (5, 1, 0, 1, 0), (5, 1, 0, 3, 1), (5, 1, 0, 2, 0), (5, 1, 0, 2, 1),
    (5, 1, 0, 3, 0), (5, 1, 0, 0, 1), (5, 1, 1, 2, 1), (5, 1, 0, 1, 1), (5, 0, 3, 0, 0), (5, 1, 2, 3, 1),
    (5, 0, 4, 0, 0), (5, 1, 2, 1, 0), (5, 1, 0, 0, 0), (5, 1, 1, 3, 1), (5, 1, 1, 0, 0), (5, 1, 1, 2, 0),
    (5, 1, 2, 2, 1), (5, 1, 2, 2, 0), (5, 1, 1, 3, 0), (5, 0, 5, 0, 0), (5, 1, 1, 0, 1), (5, 1, 2, 1, 1),
    (5, 1, 1, 1, 0), (5, 1, 2, 0, 1), (5, 1, 1, 1, 1), (5, 1, 3, 0, 0), (5, 1, 2, 3, 0), (6, 0, 0),
    (5, 1, 3, 0, 1), (5, 0, 4, 0, 1), (5, 0, 5, 0, 1), (5, 1, 2, 0, 0), (5, 0, 2, 0, 1), (5, 1, 4, 0, 0),
    (5, 1, 5, 0, 0), (5, 1, 5, 0, 1), (5, 1, 4, 0, 1), (6, 0, 1), (6, 1, 0), (6, 1, 1),
)


def layer_kernel(
    len_hbm, off_hbm, loaded_hbm, wg_hbm, wu_hbm, wd_hbm, out,
    len_t, off_t, loaded, outgoing, arrived, table, hot, w_in, wd, x, acc, hid, term, got,
    in_sem, w_sem, own_sem, spread_send, spread_recv, ag_send, ag_recv, rs_send, rs_recv,
):
    row = lax.axis_index("row")
    col = lax.axis_index("col")
    me = row * N_COL + col
    cx = lax.div(col, RING)
    cy = lax.rem(col, RING)

    inputs = [
        pltpu.make_async_copy(src, dst, in_sem.at[i])
        for i, (src, dst) in enumerate(
            ((len_hbm, len_t), (off_hbm, off_t), (loaded_hbm, loaded))
        )
    ]
    loads = [
        pltpu.make_async_copy(src, dst, w_sem.at[i])
        for i, (src, dst) in enumerate(((wg_hbm, w_in.at[0]), (wu_hbm, w_in.at[1]), (wd_hbm, wd)))
    ]
    for copy in inputs:
        copy.start()

    def partner(k):
        r = lax.rem(row + lax.div(k, N_COL), N_ROW)
        a = lax.rem(cx + lax.rem(lax.div(k, RING), RING), RING)
        b = lax.rem(cy + lax.rem(k, RING), RING)
        return r, a * RING + b

    barrier = pltpu.get_barrier_semaphore()

    def greet(k, carry):
        pl.semaphore_signal(barrier, inc=1, device_id=partner(k), device_id_type=MESH)
        return carry

    lax.fori_loop(1, SRC, greet, 0)

    for copy in inputs:
        copy.wait()
    for load in loads:
        load.start()
    lane = lax.broadcasted_iota(I32, (LOAD, LOAD), 1)
    sub = lax.broadcasted_iota(I32, (LOAD, LOAD), 0)
    pos_l = jnp.zeros((LOAD, LOAD), I32)
    pos_s = jnp.zeros((LOAD, LOAD), I32)
    own = lax.broadcasted_iota(I32, (TRAJ, SRC), 1) == me
    own_len = jnp.sum(jnp.where(own, len_t[...], 0).astype(F32), axis=1, keepdims=True).astype(I32)
    own_off = jnp.sum(jnp.where(own, off_t[...], 0).astype(F32), axis=1, keepdims=True).astype(I32)
    start = jnp.zeros((1, 1), I32)
    for j in range(TRAJ):
        end = start + own_len[j : j + 1, :]
        shift = own_off[j : j + 1, :] - start
        pos_l = jnp.where((lane >= start) & (lane < end), shift + lane, pos_l)
        pos_s = jnp.where((sub >= start) & (sub < end), shift + sub, pos_s)
        start = end
    block_l = pos_l // TOK
    block_s = pos_s // TOK
    rank = jnp.sum(
        jnp.where((block_l == block_s) & (sub < lane), 1.0, 0.0), axis=0, keepdims=True
    ).astype(I32)
    target = block_l[0:1, :] * CAP + rank
    slot = lax.broadcasted_iota(I32, (N_ROW * CAP, LOAD), 0)
    select = jnp.where(target == slot, 1.0, 0.0).astype(BF16)
    for c in range(N_COL):
        picked = jnp.dot(select, loaded[:, c * WIDTH : (c + 1) * WIDTH], preferred_element_type=F32)
        outgoing[:, c] = picked.astype(BF16).reshape(N_ROW, CAP, WIDTH)
    pl.semaphore_wait(barrier, SRC - 1)

    def spread(k, carry):
        r, c = partner(k)
        pltpu.make_async_remote_copy(
            src_ref=outgoing.at[r, c],
            dst_ref=arrived.at[me],
            send_sem=spread_send,
            recv_sem=spread_recv,
            device_id=(r, c),
            device_id_type=MESH,
        ).start()
        return carry

    lax.fori_loop(1, SRC, spread, 0)
    own_copy = pltpu.make_async_copy(outgoing.at[row, col], arrived.at[me], own_sem)
    own_copy.start()

    tok = lax.broadcasted_iota(I32, (LOAD, SRC), 0)
    pos = jnp.zeros((LOAD, SRC), I32)
    start = jnp.zeros((1, SRC), I32)
    for j in range(TRAJ):
        end = start + len_t[j : j + 1, :]
        pos = jnp.where((tok >= start) & (tok < end), off_t[j : j + 1, :] - start + tok, pos)
        start = end
    mine = pos // TOK == row
    below = jnp.where(sub > lane, 1.0, 0.0).astype(BF16)
    order = jnp.dot(below, jnp.where(mine, 1.0, 0.0).astype(BF16), preferred_element_type=F32)
    order = order.astype(I32)
    in_row = jnp.where(mine, pos % TOK + 1, 0)
    by_slot = jnp.concatenate(
        [
            jnp.sum(jnp.where(order == q, in_row, 0).astype(F32), axis=0, keepdims=True)
            for q in range(CAP)
        ],
        axis=0,
    ).astype(I32)
    wide_s = lax.broadcasted_iota(I32, (SRC, CAP), 0)
    wide_l = lax.broadcasted_iota(I32, (SRC, CAP), 1)
    spread = jnp.where(wide_s % CAP == wide_l, 1.0, 0.0).astype(BF16)
    sq_s = lax.broadcasted_iota(I32, (SRC, SRC), 0)
    sq_l = lax.broadcasted_iota(I32, (SRC, SRC), 1)
    keep = sq_l % 8 == sq_s // CAP
    group_s = lax.broadcasted_iota(I32, (CAP, SRC), 0)
    group_l = lax.broadcasted_iota(I32, (CAP, SRC), 1)
    group = jnp.where(group_l // 8 == group_s, 1.0, 0.0).astype(BF16)
    total = jnp.zeros((CAP, SRC), F32)
    for part, scale in ((by_slot // 32, 32.0), (by_slot % 32, 1.0)):
        y = jnp.dot(spread, part.astype(F32).astype(BF16), preferred_element_type=F32)
        y = jnp.where(keep, y, 0.0).astype(BF16)
        total = total + scale * lax.dot_general(
            group, y, (((1,), (1,)), ((), ())), preferred_element_type=F32
        )
    table[...] = total.astype(I32) - 1

    def place(m, carry):
        first = pl.multiple_of(m * PIECE, PIECE)
        at = lax.broadcasted_iota(I32, (PIECE, SRC), 0) + first
        for g in range(CAP):
            hot[pl.ds(first, PIECE), g * SRC : (g + 1) * SRC] = jnp.where(
                table[g : g + 1, :] == at, 1.0, 0.0
            ).astype(BF16)
        return carry

    lax.fori_loop(0, TOK // PIECE, place, 0)

    swap = lax.rem(row, 2)
    a0 = (1 - swap) * cx + swap * cy
    b0 = (1 - swap) * cy + swap * cx

    def col_of(da, db):
        a = lax.rem(a0 + da, RING)
        b = lax.rem(b0 + db, RING)
        return (1 - swap) * (a * RING + b) + swap * (b * RING + a)

    near = {
        "a+": (row, col_of(1, 0)),
        "a-": (row, col_of(3, 0)),
        "b+": (row, col_of(0, 1)),
        "b-": (row, col_of(0, 3)),
    }
    own_copy.wait()
    others = arrived.at[pl.ds(0, SRC - 1)]
    pltpu.make_async_copy(others, others, spread_recv).wait()

    def compact(m):
        def one(i, carry):
            part = pl.ds(pl.multiple_of(i * 128, 128), 128)
            from_row = pl.ds(pl.multiple_of(m * PIECE + i * 128, 128), 128)
            x[0, m, part, :] = jnp.dot(
                hot[from_row, :],
                arrived[...].reshape(SRC * CAP, WIDTH),
                preferred_element_type=F32,
            ).astype(BF16)
            return carry

        lax.fori_loop(0, PIECE // 128, one, 0)

    sends = {}
    count = [0]

    def forward(slot, m, way, to):
        copy = pltpu.make_async_remote_copy(
            src_ref=x.at[slot, m],
            dst_ref=x.at[to, m],
            send_sem=ag_send.at[count[0]],
            recv_sem=ag_recv.at[to, m],
            device_id=near[way],
            device_id_type=MESH,
        )
        count[0] += 1
        copy.start()
        sends.setdefault((slot, m), []).append(copy)

    def own_first(m):
        forward(0, m, "a-", 1 * RING)
        forward(0, m, "a+", 3 * RING)

    def own_second(m):
        forward(0, m, "b-", 1)
        forward(0, m, "b+", 3)

    def take(slot, m):
        pltpu.make_async_copy(x.at[slot, m], x.at[slot, m], ag_recv.at[slot, m]).wait()
        da, db, q = slot // RING, slot % RING, m % 2
        if db == 0:
            if da == 3 and q == 0:
                forward(slot, m, "a+", 2 * RING)
            if da == 1 and q == 1:
                forward(slot, m, "a-", 2 * RING)
            forward(slot, m, "b-", da * RING + 1)
            forward(slot, m, "b+", da * RING + 3)
        if db == 3 and q == 0:
            forward(slot, m, "b+", da * RING + 2)
        if db == 1 and q == 1:
            forward(slot, m, "b-", da * RING + 2)

    done = [0, 0]

    def gate_up(t, group):
        if sum(done) == 0:
            for load in loads[:2]:
                load.wait()
        slots = GROUPS[group]
        first, last = done[t] == 0, done[t] == len(GROUPS) - 1
        done[t] += 1
        ks = [
            pl.ds(pl.multiple_of(col_of(s // RING, s % RING) * WIDTH, WIDTH), WIDTH) for s in slots
        ]

        def one(which, carry):
            value = None
            for s, k in zip(slots, ks):
                lhs = x[s, 2 * t : 2 * t + 2].reshape(HALF, WIDTH)
                part = lax.dot_general(lhs, w_in[which, :, k], NT, preferred_element_type=F32)
                value = part if value is None else value + part
            acc[which] = value if first else acc[which] + value
            return carry

        lax.fori_loop(0, 2, one, 0)
        if last:

            def activate(i, carry):
                part = pl.ds(pl.multiple_of(i * 128, 128), 128)
                g = acc[0, part, :]
                u = acc[1, part, :]
                to = pl.ds(pl.multiple_of(t * HALF + i * 128, 128), 128)
                hid[to, :] = (g / (1.0 + jnp.exp(-g)) * u).astype(BF16)
                return carry

            lax.fori_loop(0, HALF // 128, activate, 0)

    order = [2, 6, 14, 10, 0, 1, 3, 4, 12, 5, 7, 13, 15, 8, 9, 11]
    spots = [[(s, 2 * t + q) for s in order for q in (0, 1)] for t in (0, 1)]
    started = []

    def product(slot, m):
        cols = pl.ds(pl.multiple_of(col_of(slot // RING, slot % RING) * WIDTH, WIDTH), WIDTH)

        def one(i, carry):
            part = pl.ds(pl.multiple_of(i * 128, 128), 128)
            from_row = pl.ds(pl.multiple_of(m * PIECE + i * 128, 128), 128)
            term[part, :] = jnp.dot(hid[from_row, :], wd[:, cols], preferred_element_type=F32)
            return carry

        lax.fori_loop(0, PIECE // 128, one, 0)
        return term[...]

    def landed(i, t):
        i = t * 30 + i
        pltpu.make_async_copy(got.at[i], got.at[i], rs_recv.at[i]).wait()
        return got[i].astype(F32)

    def send(value, way, to, t):
        n = len(started)
        spot = spots[t].pop(0)
        for copy in sends.pop(spot, []):
            copy.wait_send()
        x[spot[0], spot[1]] = value.astype(BF16)
        to = t * 30 + to
        copy = pltpu.make_async_remote_copy(
            src_ref=x.at[spot[0], spot[1]],
            dst_ref=got.at[to],
            send_sem=rs_send.at[n],
            recv_sem=rs_recv.at[to],
            device_id=near[way],
            device_id_type=MESH,
        )
        copy.start()
        started.append(copy)

    def chain(da, q):
        return da * 2 + q

    def plus(da, q):
        return 8 + da * 2 + q

    def minus(da, q):
        return 16 + da * 2 + q

    def scatter(t, kind, da, q):
        if kind == 0:
            send(product(da * RING + 2, 2 * t + q), "b+" if q else "b-", chain(da, q), t)
        elif kind == 1:
            if q:
                send(product(da * RING + 3, 2 * t + 1), "b-", plus(da, 1), t)
            else:
                send(product(da * RING + 1, 2 * t), "b+", minus(da, 0), t)
        elif kind == 2:
            if q:
                value = product(da * RING + 1, 2 * t + 1) + landed(chain(da, 1), t)
                send(value, "b+", minus(da, 1), t)
            else:
                value = product(da * RING + 3, 2 * t) + landed(chain(da, 0), t)
                send(value, "b-", plus(da, 0), t)
        elif kind == 3:
            send(total(t, 2, q), "a+" if q else "a-", 24 + q, t)
        elif kind == 4:
            if q:
                send(total(t, 3, 1), "a-", 27, t)
            else:
                send(total(t, 1, 0), "a+", 28, t)
        elif q:
            send(total(t, 1, 1) + landed(25, t), "a+", 29, t)
        else:
            send(total(t, 3, 0) + landed(24, t), "a-", 26, t)

    def total(t, da, q):
        return product(da * RING, 2 * t + q) + landed(plus(da, q), t) + landed(minus(da, q), t)

    def finish(t, q):
        m = 2 * t + q
        value = total(t, 0, q) + landed(26 + q, t) + landed(28 + q, t)
        out[m * PIECE : (m + 1) * PIECE, :] = value.astype(BF16)

    steps = (compact, own_first, own_second, take, gate_up, scatter, finish)
    for what, *which in PROGRAM:
        if what == 5 and not started:
            loads[2].wait()
        steps[what](*which)
    for copies in sends.values():
        for copy in copies:
            copy.wait_send()
    for copy in started:
        copy.wait_send()
    pltpu.make_async_copy(others, others, spread_send).wait()


def per_device(loaded, lengths, offsets, gate_weight, up_weight, down_weight):
    width, hidden = gate_weight.shape
    hbm = pl.BlockSpec(memory_space=pl.ANY)
    return pl.pallas_call(
        layer_kernel,
        out_shape=jax.ShapeDtypeStruct((TOK, WIDTH), BF16),
        in_specs=[hbm] * 6,
        out_specs=pl.BlockSpec(memory_space=pltpu.VMEM),
        scratch_shapes=[
            pltpu.VMEM((TRAJ, SRC), I32),
            pltpu.VMEM((TRAJ, SRC), I32),
            pltpu.VMEM((LOAD, width), BF16),
            pltpu.VMEM((N_ROW, N_COL, CAP, WIDTH), BF16),
            pltpu.VMEM((SRC, CAP, WIDTH), BF16),
            pltpu.VMEM((CAP, SRC), I32),
            pltpu.VMEM((TOK, SRC * CAP), BF16),
            pltpu.VMEM((2, hidden, width), BF16),
            pltpu.VMEM((hidden, width), BF16),
            pltpu.VMEM((N_COL, 4, PIECE, WIDTH), BF16),
            pltpu.VMEM((2, HALF, hidden), F32),
            pltpu.VMEM((TOK, hidden), BF16),
            pltpu.VMEM((PIECE, WIDTH), F32),
            pltpu.VMEM((60, PIECE, WIDTH), BF16),
            pltpu.SemaphoreType.DMA((3,)),
            pltpu.SemaphoreType.DMA((3,)),
            pltpu.SemaphoreType.DMA,
            pltpu.SemaphoreType.DMA,
            pltpu.SemaphoreType.DMA,
            pltpu.SemaphoreType.DMA((60,)),
            pltpu.SemaphoreType.DMA((N_COL, 4)),
            pltpu.SemaphoreType.DMA((60,)),
            pltpu.SemaphoreType.DMA((60,)),
        ],
        compiler_params=pltpu.CompilerParams(
            collective_id=0, has_side_effects=True, vmem_limit_bytes=60 * 1024 * 1024
        ),
        name="layer",
    )(lengths.T, offsets.T, loaded, gate_weight.T, up_weight.T, down_weight)


def solution(mesh):
    placed = (P(("row", "col"), None), P(), P(), P(None, "col"), P(None, "col"), P("col", None))
    return jax.shard_map(
        per_device, mesh=mesh, in_specs=placed, out_specs=P("row", "col"), check_vma=False
    )
```

```python
import functools

import jax
import jax.numpy as jnp
from jax import lax
from jax.experimental import pallas as pl
from jax.experimental.pallas import tpu as pltpu
from jax.sharding import PartitionSpec as P

MESH = pl.DeviceIdType.MESH
N_ROW = 8
N_COL = 16
RING = 4
LOAD = 64
CAP = 16
TRAJ = 8
TOK = 1024
HALF = 512
WIDTH = 256
PIECE = 256
STRIDE = 85
SRC = N_ROW * N_COL
NT = (((1,), (1,)), ((), ()))
I32 = jnp.int32
F32 = jnp.float32
BF16 = jnp.bfloat16
GROUPS = ((0,), (4, 12), (1, 3), (8, 2), (5, 7), (13, 15), (6, 14), (9, 11), (10,))
PROGRAM = (
    (0, 1), (1, 1), (0, 0), (0, 3), (1, 0), (1, 3), (3, 4, 1), (2, 0), (3, 12, 0), (3, 4, 0), (3, 7, 1), (2, 1),
    (3, 12, 1), (4, 0, 1), (3, 8, 1), (3, 7, 0), (3, 5, 1), (0, 2), (3, 8, 0), (3, 13, 1), (3, 1, 0),
    (3, 15, 0), (3, 11, 1), (3, 15, 1), (3, 13, 0), (3, 5, 0), (1, 2), (4, 0, 5), (3, 3, 0), (2, 3), (3, 1, 1),
    (4, 0, 4), (3, 9, 0), (4, 0, 0), (3, 11, 0), (3, 9, 1), (3, 3, 1), (3, 6, 0), (3, 14, 1), (4, 0, 7),
    (3, 14, 0), (2, 2), (3, 6, 1), (3, 4, 3), (4, 0, 2), (3, 2, 1), (3, 12, 2), (3, 1, 3), (3, 2, 0), (4, 0, 3),
    (3, 10, 0), (4, 0, 6), (3, 4, 2), (3, 10, 1), (3, 12, 3), (4, 0, 8), (5, 0, 0, 3, 0), (3, 3, 2), (4, 1, 0),
    (5, 0, 0, 0, 0), (5, 0, 0, 1, 1), (3, 7, 3), (5, 0, 0, 2, 0), (3, 1, 2), (3, 15, 2), (4, 1, 1), (3, 3, 3),
    (3, 5, 3), (3, 7, 2), (3, 15, 3), (3, 8, 2), (4, 1, 2), (5, 0, 0, 1, 0), (5, 0, 0, 3, 1), (3, 13, 2),
    (5, 0, 0, 2, 1), (3, 8, 3), (3, 2, 2), (3, 2, 3), (3, 5, 2), (4, 1, 4), (3, 13, 3), (4, 1, 3), (4, 1, 5),
    (3, 11, 2), (5, 0, 1, 0, 1), (3, 6, 2), (5, 0, 1, 3, 0), (5, 0, 2, 1, 1), (5, 0, 0, 0, 1), (5, 0, 2, 2, 0),
    (5, 0, 2, 2, 1), (5, 0, 1, 2, 0), (3, 9, 2), (3, 14, 2), (5, 0, 2, 3, 1), (3, 11, 3), (5, 0, 1, 1, 0),
    (3, 9, 3), (5, 0, 1, 1, 1), (4, 1, 7), (3, 10, 2), (5, 0, 2, 0, 0), (5, 0, 1, 0, 0), (3, 14, 3),
    (5, 0, 2, 3, 0), (3, 6, 3), (4, 1, 6), (3, 10, 3), (5, 0, 1, 3, 1), (5, 0, 1, 2, 1), (4, 1, 8),
    (5, 1, 0, 0, 0), (5, 1, 0, 2, 1), (5, 1, 0, 1, 1), (5, 1, 0, 2, 0), (5, 1, 0, 0, 1), (5, 1, 0, 3, 0),
    (5, 1, 1, 1, 0), (5, 1, 1, 1, 1), (5, 1, 0, 3, 1), (5, 0, 3, 0, 1), (5, 1, 1, 0, 1), (5, 0, 2, 1, 0),
    (5, 1, 0, 1, 0), (5, 1, 1, 2, 0), (5, 1, 2, 2, 0), (5, 1, 2, 1, 1), (5, 1, 2, 0, 0), (5, 1, 2, 2, 1),
    (5, 1, 1, 2, 1), (5, 1, 2, 3, 1), (5, 1, 1, 3, 1), (5, 1, 1, 0, 0), (5, 0, 5, 0, 1), (5, 1, 2, 1, 0),
    (5, 0, 3, 0, 0), (5, 1, 3, 0, 0), (5, 1, 1, 3, 0), (5, 1, 2, 3, 0), (5, 0, 4, 0, 0), (5, 1, 3, 0, 1),
    (5, 1, 4, 0, 1), (5, 0, 2, 0, 1), (5, 0, 4, 0, 1), (5, 1, 4, 0, 0), (5, 1, 2, 0, 1), (5, 0, 5, 0, 0),
    (5, 1, 5, 0, 0), (5, 1, 5, 0, 1), (6, 0, 0), (6, 0, 1), (6, 1, 0), (6, 1, 1),
)


def layer_kernel(
    len_hbm, off_hbm, loaded_hbm, wg_hbm, wu_hbm, wd_hbm, out,
    len_t, off_t, loaded, outgoing, arrived, table, hot, w_in, wd, x, acc, hid, term, got,
    in_sem, w_sem, own_sem, spread_send, spread_recv, ag_send, ag_recv, rs_send, rs_recv,
):
    row = lax.axis_index("row")
    col = lax.axis_index("col")
    me = row * N_COL + col
    cx = lax.div(col, RING)
    cy = lax.rem(col, RING)

    inputs = [
        pltpu.make_async_copy(src, dst, in_sem.at[i])
        for i, (src, dst) in enumerate(
            ((len_hbm, len_t), (off_hbm, off_t), (loaded_hbm, loaded))
        )
    ]
    loads = [
        pltpu.make_async_copy(src, dst, w_sem.at[i])
        for i, (src, dst) in enumerate(((wg_hbm, w_in.at[0]), (wu_hbm, w_in.at[1]), (wd_hbm, wd)))
    ]
    for copy in inputs:
        copy.start()

    def partner(k):
        k = lax.rem(k * STRIDE, SRC)
        r = lax.rem(row + lax.div(k, N_COL), N_ROW)
        a = lax.rem(cx + lax.rem(lax.div(k, RING), RING), RING)
        b = lax.rem(cy + lax.rem(k, RING), RING)
        return r, a * RING + b

    barrier = pltpu.get_barrier_semaphore()

    def each_partner(act):
        def block(i, carry):
            for j in range(8):
                act(i * 8 + j + 1)
            return carry

        lax.fori_loop(0, SRC // 8 - 1, block, 0)
        for j in range(SRC - 7, SRC):
            act(jnp.int32(j))

    def greet(k):
        pl.semaphore_signal(barrier, inc=1, device_id=partner(k), device_id_type=MESH)

    each_partner(greet)

    for copy in inputs:
        copy.wait()
    for load in loads:
        load.start()
    lane = lax.broadcasted_iota(I32, (LOAD, LOAD), 1)
    sub = lax.broadcasted_iota(I32, (LOAD, LOAD), 0)
    pos_l = jnp.zeros((LOAD, LOAD), I32)
    pos_s = jnp.zeros((LOAD, LOAD), I32)
    own = lax.broadcasted_iota(I32, (TRAJ, SRC), 1) == me
    own_len = jnp.sum(jnp.where(own, len_t[...], 0).astype(F32), axis=1, keepdims=True).astype(I32)
    own_off = jnp.sum(jnp.where(own, off_t[...], 0).astype(F32), axis=1, keepdims=True).astype(I32)
    start = jnp.zeros((1, 1), I32)
    for j in range(TRAJ):
        end = start + own_len[j : j + 1, :]
        shift = own_off[j : j + 1, :] - start
        pos_l = jnp.where((lane >= start) & (lane < end), shift + lane, pos_l)
        pos_s = jnp.where((sub >= start) & (sub < end), shift + sub, pos_s)
        start = end
    block_l = pos_l // TOK
    block_s = pos_s // TOK
    rank = jnp.sum(
        jnp.where((block_l == block_s) & (sub < lane), 1.0, 0.0), axis=0, keepdims=True
    ).astype(I32)
    target = block_l[0:1, :] * CAP + rank
    slot = lax.broadcasted_iota(I32, (N_ROW * CAP, LOAD), 0)
    select = jnp.where(target == slot, 1.0, 0.0).astype(BF16)
    for c in range(N_COL):
        picked = jnp.dot(select, loaded[:, c * WIDTH : (c + 1) * WIDTH], preferred_element_type=F32)
        outgoing[:, c] = picked.astype(BF16).reshape(N_ROW, CAP, WIDTH)
    pl.semaphore_wait(barrier, SRC - 1)

    def spread(k):
        r, c = partner(k)
        pltpu.make_async_remote_copy(
            src_ref=outgoing.at[r, c],
            dst_ref=arrived.at[me],
            send_sem=spread_send,
            recv_sem=spread_recv,
            device_id=(r, c),
            device_id_type=MESH,
        ).start()

    each_partner(spread)
    own_copy = pltpu.make_async_copy(outgoing.at[row, col], arrived.at[me], own_sem)
    own_copy.start()

    tok = lax.broadcasted_iota(I32, (LOAD, SRC), 0)
    pos = jnp.zeros((LOAD, SRC), I32)
    start = jnp.zeros((1, SRC), I32)
    for j in range(TRAJ):
        end = start + len_t[j : j + 1, :]
        pos = jnp.where((tok >= start) & (tok < end), off_t[j : j + 1, :] - start + tok, pos)
        start = end
    mine = pos // TOK == row
    below = jnp.where(sub > lane, 1.0, 0.0).astype(BF16)
    order = jnp.dot(below, jnp.where(mine, 1.0, 0.0).astype(BF16), preferred_element_type=F32)
    order = order.astype(I32)
    in_row = jnp.where(mine, pos % TOK + 1, 0)
    by_slot = jnp.concatenate(
        [
            jnp.sum(jnp.where(order == q, in_row, 0).astype(F32), axis=0, keepdims=True)
            for q in range(CAP)
        ],
        axis=0,
    ).astype(I32)
    wide_s = lax.broadcasted_iota(I32, (SRC, CAP), 0)
    wide_l = lax.broadcasted_iota(I32, (SRC, CAP), 1)
    spread = jnp.where(wide_s % CAP == wide_l, 1.0, 0.0).astype(BF16)
    sq_s = lax.broadcasted_iota(I32, (SRC, SRC), 0)
    sq_l = lax.broadcasted_iota(I32, (SRC, SRC), 1)
    keep = sq_l % 8 == sq_s // CAP
    group_s = lax.broadcasted_iota(I32, (CAP, SRC), 0)
    group_l = lax.broadcasted_iota(I32, (CAP, SRC), 1)
    group = jnp.where(group_l // 8 == group_s, 1.0, 0.0).astype(BF16)
    total = jnp.zeros((CAP, SRC), F32)
    for part, scale in ((by_slot // 32, 32.0), (by_slot % 32, 1.0)):
        y = jnp.dot(spread, part.astype(F32).astype(BF16), preferred_element_type=F32)
        y = jnp.where(keep, y, 0.0).astype(BF16)
        total = total + scale * lax.dot_general(
            group, y, (((1,), (1,)), ((), ())), preferred_element_type=F32
        )
    table[...] = total.astype(I32) - 1

    def place(m, carry):
        first = pl.multiple_of(m * PIECE, PIECE)
        at = lax.broadcasted_iota(I32, (PIECE, SRC), 0) + first
        for g in range(CAP):
            hot[pl.ds(first, PIECE), g * SRC : (g + 1) * SRC] = jnp.where(
                table[g : g + 1, :] == at, 1.0, 0.0
            ).astype(BF16)
        return carry

    lax.fori_loop(0, TOK // PIECE, place, 0)

    swap = lax.rem(row, 2)
    a0 = (1 - swap) * cx + swap * cy
    b0 = (1 - swap) * cy + swap * cx

    def col_of(da, db):
        a = lax.rem(a0 + da, RING)
        b = lax.rem(b0 + db, RING)
        return (1 - swap) * (a * RING + b) + swap * (b * RING + a)

    near = {
        "a+": (row, col_of(1, 0)),
        "a-": (row, col_of(3, 0)),
        "b+": (row, col_of(0, 1)),
        "b-": (row, col_of(0, 3)),
    }
    own_copy.wait()
    others = arrived.at[pl.ds(0, SRC - 1)]
    pltpu.make_async_copy(others, others, spread_recv).wait()

    def compact(m):
        def one(i, carry):
            part = pl.ds(pl.multiple_of(i * 128, 128), 128)
            from_row = pl.ds(pl.multiple_of(m * PIECE + i * 128, 128), 128)
            x[0, m, part, :] = jnp.dot(
                hot[from_row, :],
                arrived[...].reshape(SRC * CAP, WIDTH),
                preferred_element_type=F32,
            ).astype(BF16)
            return carry

        lax.fori_loop(0, PIECE // 128, one, 0)

    sends = {}
    count = [0]

    def forward(slot, m, way, to):
        copy = pltpu.make_async_remote_copy(
            src_ref=x.at[slot, m],
            dst_ref=x.at[to, m],
            send_sem=ag_send.at[count[0]],
            recv_sem=ag_recv.at[to, m],
            device_id=near[way],
            device_id_type=MESH,
        )
        count[0] += 1
        copy.start()
        sends.setdefault((slot, m), []).append(copy)

    def own_first(m):
        forward(0, m, "a-", 1 * RING)
        forward(0, m, "a+", 3 * RING)

    def own_second(m):
        forward(0, m, "b-", 1)
        forward(0, m, "b+", 3)

    def take(slot, m):
        pltpu.make_async_copy(x.at[slot, m], x.at[slot, m], ag_recv.at[slot, m]).wait()
        da, db, q = slot // RING, slot % RING, m % 2
        if db == 0:
            if da == 3 and q == 0:
                forward(slot, m, "a+", 2 * RING)
            if da == 1 and q == 1:
                forward(slot, m, "a-", 2 * RING)
            forward(slot, m, "b-", da * RING + 1)
            forward(slot, m, "b+", da * RING + 3)
        if db == 3 and q == 0:
            forward(slot, m, "b+", da * RING + 2)
        if db == 1 and q == 1:
            forward(slot, m, "b-", da * RING + 2)

    done = [0, 0]

    def gate_up(t, group):
        if sum(done) == 0:
            for load in loads[:2]:
                load.wait()
        slots = GROUPS[group]
        first, last = done[t] == 0, done[t] == len(GROUPS) - 1
        done[t] += 1
        ks = [
            pl.ds(pl.multiple_of(col_of(s // RING, s % RING) * WIDTH, WIDTH), WIDTH) for s in slots
        ]

        def one(which, carry):
            value = None
            for s, k in zip(slots, ks):
                lhs = x[s, 2 * t : 2 * t + 2].reshape(HALF, WIDTH)
                part = lax.dot_general(lhs, w_in[which, :, k], NT, preferred_element_type=F32)
                value = part if value is None else value + part
            acc[which] = value if first else acc[which] + value
            return carry

        lax.fori_loop(0, 2, one, 0)
        if last:

            def activate(i, carry):
                part = pl.ds(pl.multiple_of(i * 128, 128), 128)
                g = acc[0, part, :]
                u = acc[1, part, :]
                to = pl.ds(pl.multiple_of(t * HALF + i * 128, 128), 128)
                hid[to, :] = (g / (1.0 + jnp.exp(-g)) * u).astype(BF16)
                return carry

            lax.fori_loop(0, HALF // 128, activate, 0)

    order = [2, 6, 14, 10, 0, 1, 3, 4, 12, 5, 7, 13, 15, 8, 9, 11]
    spots = [[(s, 2 * t + q) for s in order for q in (0, 1)] for t in (0, 1)]
    started = []

    def product(slot, m):
        cols = pl.ds(pl.multiple_of(col_of(slot // RING, slot % RING) * WIDTH, WIDTH), WIDTH)

        def one(i, carry):
            part = pl.ds(pl.multiple_of(i * 128, 128), 128)
            from_row = pl.ds(pl.multiple_of(m * PIECE + i * 128, 128), 128)
            term[part, :] = jnp.dot(hid[from_row, :], wd[:, cols], preferred_element_type=F32)
            return carry

        lax.fori_loop(0, PIECE // 128, one, 0)
        return term[...]

    def landed(i, t):
        i = t * 30 + i
        pltpu.make_async_copy(got.at[i], got.at[i], rs_recv.at[i]).wait()
        return got[i].astype(F32)

    def send(value, way, to, t):
        n = len(started)
        spot = spots[t].pop(0)
        for copy in sends.pop(spot, []):
            copy.wait_send()
        x[spot[0], spot[1]] = value.astype(BF16)
        to = t * 30 + to
        copy = pltpu.make_async_remote_copy(
            src_ref=x.at[spot[0], spot[1]],
            dst_ref=got.at[to],
            send_sem=rs_send.at[n],
            recv_sem=rs_recv.at[to],
            device_id=near[way],
            device_id_type=MESH,
        )
        copy.start()
        started.append(copy)

    def chain(da, q):
        return da * 2 + q

    def plus(da, q):
        return 8 + da * 2 + q

    def minus(da, q):
        return 16 + da * 2 + q

    def scatter(t, kind, da, q):
        if kind == 0:
            send(product(da * RING + 2, 2 * t + q), "b+" if q else "b-", chain(da, q), t)
        elif kind == 1:
            if q:
                send(product(da * RING + 3, 2 * t + 1), "b-", plus(da, 1), t)
            else:
                send(product(da * RING + 1, 2 * t), "b+", minus(da, 0), t)
        elif kind == 2:
            if q:
                value = product(da * RING + 1, 2 * t + 1) + landed(chain(da, 1), t)
                send(value, "b+", minus(da, 1), t)
            else:
                value = product(da * RING + 3, 2 * t) + landed(chain(da, 0), t)
                send(value, "b-", plus(da, 0), t)
        elif kind == 3:
            send(total(t, 2, q), "a+" if q else "a-", 24 + q, t)
        elif kind == 4:
            if q:
                send(total(t, 3, 1), "a-", 27, t)
            else:
                send(total(t, 1, 0), "a+", 28, t)
        elif q:
            send(total(t, 1, 1) + landed(25, t), "a+", 29, t)
        else:
            send(total(t, 3, 0) + landed(24, t), "a-", 26, t)

    def total(t, da, q):
        return product(da * RING, 2 * t + q) + landed(plus(da, q), t) + landed(minus(da, q), t)

    def finish(t, q):
        m = 2 * t + q
        value = total(t, 0, q) + landed(26 + q, t) + landed(28 + q, t)
        out[m * PIECE : (m + 1) * PIECE, :] = value.astype(BF16)

    steps = (compact, own_first, own_second, take, gate_up, scatter, finish)
    for what, *which in PROGRAM:
        if what == 5 and not started:
            loads[2].wait()
        steps[what](*which)
    for copies in sends.values():
        for copy in copies:
            copy.wait_send()
    for copy in started:
        copy.wait_send()
    pltpu.make_async_copy(others, others, spread_send).wait()


def per_device(loaded, lengths, offsets, gate_weight, up_weight, down_weight):
    width, hidden = gate_weight.shape
    hbm = pl.BlockSpec(memory_space=pl.ANY)
    return pl.pallas_call(
        layer_kernel,
        out_shape=jax.ShapeDtypeStruct((TOK, WIDTH), BF16),
        in_specs=[hbm] * 6,
        out_specs=pl.BlockSpec(memory_space=pltpu.VMEM),
        scratch_shapes=[
            pltpu.VMEM((TRAJ, SRC), I32),
            pltpu.VMEM((TRAJ, SRC), I32),
            pltpu.VMEM((LOAD, width), BF16),
            pltpu.VMEM((N_ROW, N_COL, CAP, WIDTH), BF16),
            pltpu.VMEM((SRC, CAP, WIDTH), BF16),
            pltpu.VMEM((CAP, SRC), I32),
            pltpu.VMEM((TOK, SRC * CAP), BF16),
            pltpu.VMEM((2, hidden, width), BF16),
            pltpu.VMEM((hidden, width), BF16),
            pltpu.VMEM((N_COL, 4, PIECE, WIDTH), BF16),
            pltpu.VMEM((2, HALF, hidden), F32),
            pltpu.VMEM((TOK, hidden), BF16),
            pltpu.VMEM((PIECE, WIDTH), F32),
            pltpu.VMEM((60, PIECE, WIDTH), BF16),
            pltpu.SemaphoreType.DMA((3,)),
            pltpu.SemaphoreType.DMA((3,)),
            pltpu.SemaphoreType.DMA,
            pltpu.SemaphoreType.DMA,
            pltpu.SemaphoreType.DMA,
            pltpu.SemaphoreType.DMA((60,)),
            pltpu.SemaphoreType.DMA((N_COL, 4)),
            pltpu.SemaphoreType.DMA((60,)),
            pltpu.SemaphoreType.DMA((60,)),
        ],
        compiler_params=pltpu.CompilerParams(
            collective_id=0, has_side_effects=True, vmem_limit_bytes=60 * 1024 * 1024
        ),
        name="layer",
    )(lengths.T, offsets.T, loaded, gate_weight.T, up_weight.T, down_weight)


def solution(mesh):
    placed = (P(("row", "col"), None), P(), P(), P(None, "col"), P(None, "col"), P("col", None))
    return jax.shard_map(
        per_device, mesh=mesh, in_specs=placed, out_specs=P("row", "col"), check_vma=False
    )
```

```python
import functools

import jax
import jax.numpy as jnp
from jax import lax
from jax.experimental import pallas as pl
from jax.experimental.pallas import tpu as pltpu
from jax.sharding import PartitionSpec as P

MESH = pl.DeviceIdType.MESH
N_ROW = 8
N_COL = 16
RING = 4
LOAD = 64
CAP = 16
TRAJ = 8
TOK = 1024
HALF = 512
WIDTH = 256
PIECE = 256
STRIDE = 85
SRC = N_ROW * N_COL
NT = (((1,), (1,)), ((), ()))
I32 = jnp.int32
F32 = jnp.float32
BF16 = jnp.bfloat16
GROUPS = ((0,), (4, 12), (1, 3), (8, 2), (5, 7), (13, 15), (6, 14), (9, 11), (10,))
PROGRAM = (
    (0, 1), (1, 1), (0, 0), (0, 3), (1, 0), (1, 3), (3, 4, 1), (2, 0), (3, 12, 0), (3, 4, 0), (3, 7, 1), (2, 1),
    (3, 12, 1), (4, 0, 1), (3, 8, 1), (3, 7, 0), (3, 5, 1), (0, 2), (3, 8, 0), (3, 13, 1), (3, 1, 0),
    (3, 15, 0), (3, 11, 1), (3, 15, 1), (3, 13, 0), (3, 5, 0), (1, 2), (4, 0, 5), (3, 3, 0), (2, 3), (3, 1, 1),
    (4, 0, 4), (3, 9, 0), (4, 0, 0), (3, 11, 0), (3, 9, 1), (3, 3, 1), (3, 6, 0), (3, 14, 1), (4, 0, 7),
    (3, 14, 0), (2, 2), (3, 6, 1), (3, 4, 3), (4, 0, 2), (3, 2, 1), (3, 12, 2), (3, 1, 3), (3, 2, 0), (4, 0, 3),
    (3, 10, 0), (4, 0, 6), (3, 4, 2), (3, 10, 1), (3, 12, 3), (4, 0, 8), (5, 0, 0, 3, 0), (3, 3, 2), (4, 1, 0),
    (5, 0, 0, 0, 0), (5, 0, 0, 1, 1), (3, 7, 3), (5, 0, 0, 2, 0), (3, 1, 2), (3, 15, 2), (4, 1, 1), (3, 3, 3),
    (3, 5, 3), (3, 7, 2), (3, 15, 3), (3, 8, 2), (4, 1, 2), (5, 0, 0, 1, 0), (5, 0, 0, 3, 1), (3, 13, 2),
    (5, 0, 0, 2, 1), (3, 8, 3), (3, 2, 2), (3, 2, 3), (3, 5, 2), (4, 1, 4), (3, 13, 3), (4, 1, 3), (4, 1, 5),
    (3, 11, 2), (5, 0, 1, 0, 1), (3, 6, 2), (5, 0, 1, 3, 0), (5, 0, 2, 1, 1), (5, 0, 0, 0, 1), (5, 0, 2, 2, 0),
    (5, 0, 2, 2, 1), (5, 0, 1, 2, 0), (3, 9, 2), (3, 14, 2), (5, 0, 2, 3, 1), (3, 11, 3), (5, 0, 1, 1, 0),
    (3, 9, 3), (5, 0, 1, 1, 1), (4, 1, 7), (3, 10, 2), (5, 0, 2, 0, 0), (5, 0, 1, 0, 0), (3, 14, 3),
    (5, 0, 2, 3, 0), (3, 6, 3), (4, 1, 6), (3, 10, 3), (5, 0, 1, 3, 1), (5, 0, 1, 2, 1), (4, 1, 8),
    (5, 1, 0, 0, 0), (5, 1, 0, 2, 1), (5, 1, 0, 1, 1), (5, 1, 0, 2, 0), (5, 1, 0, 0, 1), (5, 1, 0, 3, 0),
    (5, 1, 1, 1, 0), (5, 1, 1, 1, 1), (5, 1, 0, 3, 1), (5, 0, 3, 0, 1), (5, 1, 1, 0, 1), (5, 0, 2, 1, 0),
    (5, 1, 0, 1, 0), (5, 1, 1, 2, 0), (5, 1, 2, 2, 0), (5, 1, 2, 1, 1), (5, 1, 2, 0, 0), (5, 1, 2, 2, 1),
    (5, 1, 1, 2, 1), (5, 1, 2, 3, 1), (5, 1, 1, 3, 1), (5, 1, 1, 0, 0), (5, 0, 5, 0, 1), (5, 1, 2, 1, 0),
    (5, 0, 3, 0, 0), (5, 1, 3, 0, 0), (5, 1, 1, 3, 0), (5, 1, 2, 3, 0), (5, 0, 4, 0, 0), (5, 1, 3, 0, 1),
    (5, 1, 4, 0, 1), (5, 0, 2, 0, 1), (5, 0, 4, 0, 1), (5, 1, 4, 0, 0), (5, 1, 2, 0, 1), (5, 0, 5, 0, 0),
    (5, 1, 5, 0, 0), (5, 1, 5, 0, 1), (6, 0, 0), (6, 0, 1), (6, 1, 0), (6, 1, 1),
)


def layer_kernel(
    len_t, off_t, loaded_hbm, wg_hbm, wu_hbm, wd_hbm, out,
    loaded, outgoing, arrived, table, hot, w_in, wd, x, acc, hid, term, got,
    in_sem, w_sem, own_sem, spread_send, spread_recv, ag_send, ag_recv, rs_send, rs_recv,
):
    row = lax.axis_index("row")
    col = lax.axis_index("col")
    me = row * N_COL + col
    cx = lax.div(col, RING)
    cy = lax.rem(col, RING)

    inputs = [
        pltpu.make_async_copy(src, dst, in_sem.at[i])
        for i, (src, dst) in enumerate(
            ((loaded_hbm, loaded),)
        )
    ]
    loads = [
        pltpu.make_async_copy(src, dst, w_sem.at[i])
        for i, (src, dst) in enumerate(((wg_hbm, w_in.at[0]), (wu_hbm, w_in.at[1]), (wd_hbm, wd)))
    ]
    for copy in inputs:
        copy.start()

    def partner(k):
        k = lax.rem(k * STRIDE, SRC)
        r = lax.rem(row + lax.div(k, N_COL), N_ROW)
        a = lax.rem(cx + lax.rem(lax.div(k, RING), RING), RING)
        b = lax.rem(cy + lax.rem(k, RING), RING)
        return r, a * RING + b

    barrier = pltpu.get_barrier_semaphore()

    def each_partner(act):
        def block(i, carry):
            for j in range(8):
                act(i * 8 + j + 1)
            return carry

        lax.fori_loop(0, SRC // 8 - 1, block, 0)
        for j in range(SRC - 7, SRC):
            act(jnp.int32(j))

    def greet(k):
        pl.semaphore_signal(barrier, inc=1, device_id=partner(k), device_id_type=MESH)

    each_partner(greet)

    for copy in inputs:
        copy.wait()
    for load in loads:
        load.start()
    lane = lax.broadcasted_iota(I32, (LOAD, LOAD), 1)
    sub = lax.broadcasted_iota(I32, (LOAD, LOAD), 0)
    pos_l = jnp.zeros((LOAD, LOAD), I32)
    pos_s = jnp.zeros((LOAD, LOAD), I32)
    own = lax.broadcasted_iota(I32, (TRAJ, SRC), 1) == me
    own_len = jnp.sum(jnp.where(own, len_t[...], 0).astype(F32), axis=1, keepdims=True).astype(I32)
    own_off = jnp.sum(jnp.where(own, off_t[...], 0).astype(F32), axis=1, keepdims=True).astype(I32)
    start = jnp.zeros((1, 1), I32)
    for j in range(TRAJ):
        end = start + own_len[j : j + 1, :]
        shift = own_off[j : j + 1, :] - start
        pos_l = jnp.where((lane >= start) & (lane < end), shift + lane, pos_l)
        pos_s = jnp.where((sub >= start) & (sub < end), shift + sub, pos_s)
        start = end
    block_l = pos_l // TOK
    block_s = pos_s // TOK
    rank = jnp.sum(
        jnp.where((block_l == block_s) & (sub < lane), 1.0, 0.0), axis=0, keepdims=True
    ).astype(I32)
    target = block_l[0:1, :] * CAP + rank
    slot = lax.broadcasted_iota(I32, (N_ROW * CAP, LOAD), 0)
    select = jnp.where(target == slot, 1.0, 0.0).astype(BF16)
    for c in range(N_COL):
        picked = jnp.dot(select, loaded[:, c * WIDTH : (c + 1) * WIDTH], preferred_element_type=F32)
        outgoing[:, c] = picked.astype(BF16).reshape(N_ROW, CAP, WIDTH)
    pl.semaphore_wait(barrier, SRC - 1)

    def spread(k):
        r, c = partner(k)
        pltpu.make_async_remote_copy(
            src_ref=outgoing.at[r, c],
            dst_ref=arrived.at[me],
            send_sem=spread_send,
            recv_sem=spread_recv,
            device_id=(r, c),
            device_id_type=MESH,
        ).start()

    each_partner(spread)
    own_copy = pltpu.make_async_copy(outgoing.at[row, col], arrived.at[me], own_sem)
    own_copy.start()

    tok = lax.broadcasted_iota(I32, (LOAD, SRC), 0)
    pos = jnp.zeros((LOAD, SRC), I32)
    start = jnp.zeros((1, SRC), I32)
    for j in range(TRAJ):
        end = start + len_t[j : j + 1, :]
        pos = jnp.where((tok >= start) & (tok < end), off_t[j : j + 1, :] - start + tok, pos)
        start = end
    mine = pos // TOK == row
    below = jnp.where(sub > lane, 1.0, 0.0).astype(BF16)
    order = jnp.dot(below, jnp.where(mine, 1.0, 0.0).astype(BF16), preferred_element_type=F32)
    order = order.astype(I32)
    in_row = jnp.where(mine, pos % TOK + 1, 0)
    by_slot = jnp.concatenate(
        [
            jnp.sum(jnp.where(order == q, in_row, 0).astype(F32), axis=0, keepdims=True)
            for q in range(CAP)
        ],
        axis=0,
    ).astype(I32)
    wide_s = lax.broadcasted_iota(I32, (SRC, CAP), 0)
    wide_l = lax.broadcasted_iota(I32, (SRC, CAP), 1)
    spread = jnp.where(wide_s % CAP == wide_l, 1.0, 0.0).astype(BF16)
    sq_s = lax.broadcasted_iota(I32, (SRC, SRC), 0)
    sq_l = lax.broadcasted_iota(I32, (SRC, SRC), 1)
    keep = sq_l % 8 == sq_s // CAP
    group_s = lax.broadcasted_iota(I32, (CAP, SRC), 0)
    group_l = lax.broadcasted_iota(I32, (CAP, SRC), 1)
    group = jnp.where(group_l // 8 == group_s, 1.0, 0.0).astype(BF16)
    total = jnp.zeros((CAP, SRC), F32)
    for part, scale in ((by_slot // 32, 32.0), (by_slot % 32, 1.0)):
        y = jnp.dot(spread, part.astype(F32).astype(BF16), preferred_element_type=F32)
        y = jnp.where(keep, y, 0.0).astype(BF16)
        total = total + scale * lax.dot_general(
            group, y, (((1,), (1,)), ((), ())), preferred_element_type=F32
        )
    table[...] = total.astype(I32) - 1

    def place(m, carry):
        first = pl.multiple_of(m * PIECE, PIECE)
        at = lax.broadcasted_iota(I32, (PIECE, SRC), 0) + first
        for g in range(CAP):
            hot[pl.ds(first, PIECE), g * SRC : (g + 1) * SRC] = jnp.where(
                table[g : g + 1, :] == at, 1.0, 0.0
            ).astype(BF16)
        return carry

    lax.fori_loop(0, TOK // PIECE, place, 0)

    swap = lax.rem(row, 2)
    a0 = (1 - swap) * cx + swap * cy
    b0 = (1 - swap) * cy + swap * cx

    def col_of(da, db):
        a = lax.rem(a0 + da, RING)
        b = lax.rem(b0 + db, RING)
        return (1 - swap) * (a * RING + b) + swap * (b * RING + a)

    near = {
        "a+": (row, col_of(1, 0)),
        "a-": (row, col_of(3, 0)),
        "b+": (row, col_of(0, 1)),
        "b-": (row, col_of(0, 3)),
    }
    own_copy.wait()
    others = arrived.at[pl.ds(0, SRC - 1)]
    pltpu.make_async_copy(others, others, spread_recv).wait()

    def compact(m):
        def one(i, carry):
            part = pl.ds(pl.multiple_of(i * 128, 128), 128)
            from_row = pl.ds(pl.multiple_of(m * PIECE + i * 128, 128), 128)
            x[0, m, part, :] = jnp.dot(
                hot[from_row, :],
                arrived[...].reshape(SRC * CAP, WIDTH),
                preferred_element_type=F32,
            ).astype(BF16)
            return carry

        lax.fori_loop(0, PIECE // 128, one, 0)

    sends = {}
    count = [0]

    def forward(slot, m, way, to):
        copy = pltpu.make_async_remote_copy(
            src_ref=x.at[slot, m],
            dst_ref=x.at[to, m],
            send_sem=ag_send.at[count[0]],
            recv_sem=ag_recv.at[to, m],
            device_id=near[way],
            device_id_type=MESH,
        )
        count[0] += 1
        copy.start()
        sends.setdefault((slot, m), []).append(copy)

    def own_first(m):
        forward(0, m, "a-", 1 * RING)
        forward(0, m, "a+", 3 * RING)

    def own_second(m):
        forward(0, m, "b-", 1)
        forward(0, m, "b+", 3)

    def take(slot, m):
        pltpu.make_async_copy(x.at[slot, m], x.at[slot, m], ag_recv.at[slot, m]).wait()
        da, db, q = slot // RING, slot % RING, m % 2
        if db == 0:
            if da == 3 and q == 0:
                forward(slot, m, "a+", 2 * RING)
            if da == 1 and q == 1:
                forward(slot, m, "a-", 2 * RING)
            forward(slot, m, "b-", da * RING + 1)
            forward(slot, m, "b+", da * RING + 3)
        if db == 3 and q == 0:
            forward(slot, m, "b+", da * RING + 2)
        if db == 1 and q == 1:
            forward(slot, m, "b-", da * RING + 2)

    done = [0, 0]

    def gate_up(t, group):
        if sum(done) == 0:
            for load in loads[:2]:
                load.wait()
        slots = GROUPS[group]
        first, last = done[t] == 0, done[t] == len(GROUPS) - 1
        done[t] += 1
        ks = [
            pl.ds(pl.multiple_of(col_of(s // RING, s % RING) * WIDTH, WIDTH), WIDTH) for s in slots
        ]

        def one(which, carry):
            value = None
            for s, k in zip(slots, ks):
                lhs = x[s, 2 * t : 2 * t + 2].reshape(HALF, WIDTH)
                part = lax.dot_general(lhs, w_in[which, :, k], NT, preferred_element_type=F32)
                value = part if value is None else value + part
            acc[which] = value if first else acc[which] + value
            return carry

        lax.fori_loop(0, 2, one, 0)
        if last:

            def activate(i, carry):
                part = pl.ds(pl.multiple_of(i * 128, 128), 128)
                g = acc[0, part, :]
                u = acc[1, part, :]
                to = pl.ds(pl.multiple_of(t * HALF + i * 128, 128), 128)
                hid[to, :] = (g / (1.0 + jnp.exp(-g)) * u).astype(BF16)
                return carry

            lax.fori_loop(0, HALF // 128, activate, 0)

    order = [2, 6, 14, 10, 0, 1, 3, 4, 12, 5, 7, 13, 15, 8, 9, 11]
    spots = [[(s, 2 * t + q) for s in order for q in (0, 1)] for t in (0, 1)]
    started = []

    def product(slot, m):
        cols = pl.ds(pl.multiple_of(col_of(slot // RING, slot % RING) * WIDTH, WIDTH), WIDTH)

        def one(i, carry):
            part = pl.ds(pl.multiple_of(i * 128, 128), 128)
            from_row = pl.ds(pl.multiple_of(m * PIECE + i * 128, 128), 128)
            term[part, :] = jnp.dot(hid[from_row, :], wd[:, cols], preferred_element_type=F32)
            return carry

        lax.fori_loop(0, PIECE // 128, one, 0)
        return term[...]

    def landed(i, t):
        i = t * 30 + i
        pltpu.make_async_copy(got.at[i], got.at[i], rs_recv.at[i]).wait()
        return got[i].astype(F32)

    def send(value, way, to, t):
        n = len(started)
        spot = spots[t].pop(0)
        for copy in sends.pop(spot, []):
            copy.wait_send()
        x[spot[0], spot[1]] = value.astype(BF16)
        to = t * 30 + to
        copy = pltpu.make_async_remote_copy(
            src_ref=x.at[spot[0], spot[1]],
            dst_ref=got.at[to],
            send_sem=rs_send.at[n],
            recv_sem=rs_recv.at[to],
            device_id=near[way],
            device_id_type=MESH,
        )
        copy.start()
        started.append(copy)

    def chain(da, q):
        return da * 2 + q

    def plus(da, q):
        return 8 + da * 2 + q

    def minus(da, q):
        return 16 + da * 2 + q

    def scatter(t, kind, da, q):
        if kind == 0:
            send(product(da * RING + 2, 2 * t + q), "b+" if q else "b-", chain(da, q), t)
        elif kind == 1:
            if q:
                send(product(da * RING + 3, 2 * t + 1), "b-", plus(da, 1), t)
            else:
                send(product(da * RING + 1, 2 * t), "b+", minus(da, 0), t)
        elif kind == 2:
            if q:
                value = product(da * RING + 1, 2 * t + 1) + landed(chain(da, 1), t)
                send(value, "b+", minus(da, 1), t)
            else:
                value = product(da * RING + 3, 2 * t) + landed(chain(da, 0), t)
                send(value, "b-", plus(da, 0), t)
        elif kind == 3:
            send(total(t, 2, q), "a+" if q else "a-", 24 + q, t)
        elif kind == 4:
            if q:
                send(total(t, 3, 1), "a-", 27, t)
            else:
                send(total(t, 1, 0), "a+", 28, t)
        elif q:
            send(total(t, 1, 1) + landed(25, t), "a+", 29, t)
        else:
            send(total(t, 3, 0) + landed(24, t), "a-", 26, t)

    def total(t, da, q):
        return product(da * RING, 2 * t + q) + landed(plus(da, q), t) + landed(minus(da, q), t)

    def finish(t, q):
        m = 2 * t + q
        value = total(t, 0, q) + landed(26 + q, t) + landed(28 + q, t)
        out[m * PIECE : (m + 1) * PIECE, :] = value.astype(BF16)

    steps = (compact, own_first, own_second, take, gate_up, scatter, finish)
    for what, *which in PROGRAM:
        if what == 5 and not started:
            loads[2].wait()
        steps[what](*which)
    for copies in sends.values():
        for copy in copies:
            copy.wait_send()
    for copy in started:
        copy.wait_send()
    pltpu.make_async_copy(others, others, spread_send).wait()


def per_device(loaded, lengths, offsets, gate_weight, up_weight, down_weight):
    width, hidden = gate_weight.shape
    hbm = pl.BlockSpec(memory_space=pltpu.HBM)
    vmem = pl.BlockSpec(memory_space=pltpu.VMEM)
    return pl.pallas_call(
        layer_kernel,
        out_shape=jax.ShapeDtypeStruct((TOK, WIDTH), BF16),
        in_specs=[vmem] * 2 + [hbm] * 4,
        out_specs=pl.BlockSpec(memory_space=pltpu.VMEM),
        scratch_shapes=[
            pltpu.VMEM((LOAD, width), BF16),
            pltpu.VMEM((N_ROW, N_COL, CAP, WIDTH), BF16),
            pltpu.VMEM((SRC, CAP, WIDTH), BF16),
            pltpu.VMEM((CAP, SRC), I32),
            pltpu.VMEM((TOK, SRC * CAP), BF16),
            pltpu.VMEM((2, hidden, width), BF16),
            pltpu.VMEM((hidden, width), BF16),
            pltpu.VMEM((N_COL, 4, PIECE, WIDTH), BF16),
            pltpu.VMEM((2, HALF, hidden), F32),
            pltpu.VMEM((TOK, hidden), BF16),
            pltpu.VMEM((PIECE, WIDTH), F32),
            pltpu.VMEM((60, PIECE, WIDTH), BF16),
            pltpu.SemaphoreType.DMA((1,)),
            pltpu.SemaphoreType.DMA((3,)),
            pltpu.SemaphoreType.DMA,
            pltpu.SemaphoreType.DMA,
            pltpu.SemaphoreType.DMA,
            pltpu.SemaphoreType.DMA((60,)),
            pltpu.SemaphoreType.DMA((N_COL, 4)),
            pltpu.SemaphoreType.DMA((60,)),
            pltpu.SemaphoreType.DMA((60,)),
        ],
        compiler_params=pltpu.CompilerParams(
            collective_id=0, has_side_effects=True, vmem_limit_bytes=53 * 1024 * 1024
        ),
        name="layer",
    )(lengths.T, offsets.T, loaded, gate_weight.T, up_weight.T, down_weight)


def solution(mesh):
    placed = (P(("row", "col"), None), P(), P(), P(None, "col"), P(None, "col"), P("col", None))
    return jax.shard_map(
        per_device, mesh=mesh, in_specs=placed, out_specs=P("row", "col"), check_vma=False
    )
```
